512 devices in a mesh: ctx: 64 (over y_lo, z, core), tp: 8 (over x, y_hi).
Axes of the slice: x: 4, y: 8 (y_hi: 2, y_lo: 4; y = y_hi * 4 + y_lo), z: 8, core: 2. Of those that a mesh axis runs over, the one named last changes fastest.
Arguments:
- latent_tokens: float32 [8192, 64], P('ctx'), may hold values from -6 to 6
- positions: int32 [8192], P('ctx'), may hold values from 0 to 8191, as said below
- queries: bfloat16 [8192, 2048], P('ctx', 'tp'), may hold values from -12 to 12
- key_states: bfloat16 [8192, 2048], P('ctx', 'tp'), may hold values from -12 to 12
- value_states: bfloat16 [8192, 2048], P('ctx', 'tp'), may hold values from -6 to 6
- attention_out: bfloat16 [8192, 2048], P('ctx', 'tp'), may hold values from -6 to 6
- projection: bfloat16 [2048, 128], P('tp'), may hold values from -0.125 to 0.125
Outputs:
- query_grad: bfloat16 [8192, 2048], P('ctx', 'tp')
- key_grad: bfloat16 [8192, 2048], P('ctx', 'tp')
- value_grad: bfloat16 [8192, 2048], P('ctx', 'tp')
The draws below stay inside these ranges and needn't reach their ends.
Inputs may be any that keep to these rules, and one draw needn't show every extreme that they name: A permutation of the positions 0 to 8191. The sequence is cut into 128 blocks of 64 consecutive positions, block b holding positions b * 64 to (b + 1) * 64 - 1. Rows k * 128 to (k + 1) * 128 - 1 hold one block b below 64 in increasing order, then block 127 - b in increasing order; each such b appears in exactly one such group of rows.
All inputs are finite; a program needn't handle non-finite values.
Results may differ from the reference program's by a relative error of at most 0.022.
Values may be sent and summed in bfloat16 or wider, within the bound.
No kernel may reach another device: no remote copies, remote signals or barrier semaphores. Data moves between devices by JAX's collectives and lax.ppermute only.
A program may use at most 128 MiB of HBM per device.

```python
import jax
import jax.numpy as jnp
from jax import lax

HEADS = 16
HEAD = 128
LAT = 64
SPAN = 64
TOKENS = 8192
HD = 2048
N_CTX = 64


def draw_positions(key, part):
    key = jax.random.fold_in(key, 11)
    order = jax.random.permutation(key, N_CTX)
    offsets = jnp.arange(SPAN)
    early = order[:, None] * SPAN + offsets[None, :]
    later = (2 * N_CTX - 1 - order)[:, None] * SPAN + offsets[None, :]
    return jnp.concatenate([early, later], axis=1).reshape(-1).astype(jnp.int32)


def draw_queries(key, part):
    own_key = jax.random.fold_in(key, 1)
    result = jnp.clip(jax.random.normal(own_key, (TOKENS, HEADS * HEAD), jnp.float32), -6.0, 6.0)
    return result.astype(jnp.bfloat16)


def draw_key_states(key, part):
    own_key = jax.random.fold_in(key, 2)
    result = jnp.clip(jax.random.normal(own_key, (TOKENS, HEADS * HEAD), jnp.float32), -6.0, 6.0)
    return result.astype(jnp.bfloat16)


def block_scale(stream_key, extent, split, least, largest):
    level = 1.0
    for position, parts in split:
        draws = jax.random.uniform(jax.random.fold_in(jax.random.fold_in(stream_key, 6), position), (parts,), jnp.float32, least / len(split), largest / len(split))
        level = level * jnp.repeat(jnp.exp(draws), extent[position] // parts).reshape((-1,) + (1,) * (len(extent) - 1 - position))
    return level


def noise(stream_key, extent, scale, bound, pieces=(), kind=jnp.bfloat16):
    values = jax.random.normal(stream_key, extent, jnp.float32) * scale
    if len(pieces) > 0:
        values = block_scale(stream_key, extent, pieces, -0.22, 0.18) * values
    return jnp.clip(values, min=-bound, max=bound).astype(kind)


def setup_inputs(seed: int = 0) -> dict:
    seeds = jax.random.split(jax.random.key(seed), 8)
    latent_tokens = noise(seeds[0], (TOKENS, LAT), 1.0, 6.0, ((0, 64),), jnp.float32)
    positions = draw_positions(jax.random.fold_in(seeds[7], 71), 0)
    queries = draw_queries(jax.random.fold_in(seeds[7], 71), 0)
    key_states = draw_key_states(jax.random.fold_in(seeds[7], 71), 0)
    value_states = noise(seeds[4], (TOKENS, HD), 1.0, 6.0, ((0, 64), (1, 8)))
    attention_out = noise(seeds[5], (TOKENS, HD), 1.0, 6.0, ((0, 64), (1, 8)))
    projection = noise(seeds[6], (HD, 2 * LAT), HD ** -0.5, 0.125, ((0, 8),))
    return {"latent_tokens": latent_tokens, "positions": positions, "queries": queries, "key_states": key_states, "value_states": value_states, "attention_out": attention_out, "projection": projection}


def coupling_grad(latent_tokens, coupled, projection):
    shifts = coupled[:, :LAT]
    log_scale = coupled[:, LAT:]
    damping = jnp.exp(-log_scale)
    normed = (latent_tokens - shifts) * damping
    upstream = jnp.concatenate([-normed * damping, 1.0 - normed * normed], axis=1).astype(jnp.bfloat16)
    return jnp.dot(upstream, projection.T, preferred_element_type=jnp.float32).astype(jnp.bfloat16)

def by_heads(values):
    return values.reshape(TOKENS, HEADS, HEAD).transpose(1, 0, 2)

def from_heads(values):
    return values.transpose(1, 0, 2).reshape(TOKENS, HEADS * HEAD)

def reference(latent_tokens, positions, queries, key_states, value_states, attention_out, projection):
    coupled = jnp.dot(attention_out, projection, preferred_element_type=jnp.float32)
    out_grad = coupling_grad(latent_tokens, coupled, projection)
    row_delta = lax.optimization_barrier(jnp.sum(by_heads(out_grad).astype(jnp.float32) * by_heads(attention_out).astype(jnp.float32), axis=2))
    allowed = positions[None, :] <= positions[:, None]
    factor = HEAD ** (-0.5)

    def one_head(inputs_head):
        query_rows, key_rows, value_rows, grad_rows, delta_rows = inputs_head
        scores = jnp.dot(query_rows, key_rows.T, preferred_element_type=jnp.float32) * factor
        masked = jnp.where(allowed, scores, -jnp.inf)
        lse = jax.nn.logsumexp(masked, axis=1)
        probs = jnp.exp(masked - lse[:, None])
        prob_grad = jnp.dot(grad_rows, value_rows.T, preferred_element_type=jnp.float32)
        score_grad = probs * (prob_grad - delta_rows[:, None])
        query_out = jnp.dot(score_grad, key_rows.astype(jnp.float32), precision=lax.Precision.HIGHEST) * factor
        value_out = jnp.dot(probs.astype(jnp.bfloat16).T, grad_rows, preferred_element_type=jnp.float32)
        key_out = jnp.dot(score_grad.astype(jnp.bfloat16).T, query_rows, preferred_element_type=jnp.float32) * factor
        return (query_out.astype(jnp.bfloat16), key_out.astype(jnp.bfloat16), value_out.astype(jnp.bfloat16))
    grads = lax.map(one_head, (by_heads(queries), by_heads(key_states), by_heads(value_states), by_heads(out_grad), row_delta))
    return (from_heads(grads[0]), from_heads(grads[1]), from_heads(grads[2]))
```

```python
import functools

import jax
import jax.numpy as jnp
from jax import lax
from jax.experimental import pallas as pl
from jax.experimental.pallas import tpu as pltpu
from jax.sharding import Mesh, PartitionSpec as P

HEAD = 128
SPAN = 64
NZ, NY, NC = 8, 4, 2
LOG2E = 1.4426950408889634
FACTOR = HEAD ** (-0.5)
SCALE = FACTOR * LOG2E
MASKED = -(2.0**100)
F32 = jnp.float32
BF16 = jnp.bfloat16
NT = (((1,), (1,)), ((), ()))
MIB = 1 << 20


def dot_nt(a, b):
    return lax.dot_general(a, b, NT, preferred_element_type=F32)


def dot(a, b):
    return jnp.dot(a, b, preferred_element_type=F32)


def prep_kernel(pos_ref, q_ref, k_ref, v_ref, o_ref, proj_ref, qpay_ref, kvpay_ref, part_ref):
    block = lax.shift_right_logical(pos_ref[0], 6).astype(F32)
    tag = jnp.full((16, 256), block, F32).astype(BF16)
    q = q_ref[...]
    for i in range(NZ):
        qpay_ref[i, 0:128, :] = q
        qpay_ref[i, 128:144, :] = tag
    kvpay_ref[0:128, :] = k_ref[...]
    kvpay_ref[128:256, :] = v_ref[...]
    kvpay_ref[256:272, :] = tag
    part_ref[...] = dot(o_ref[...], proj_ref[...])


def query_positions(qg_ref):
    lane = lax.broadcasted_iota(jnp.int32, (1, 128), 1)
    low = lane < SPAN
    row = (lane & (SPAN - 1)).astype(F32)
    early, late = [], []
    for p in range(NZ // 2):
        first = qg_ref[2 * p, 128:144, 0:128].astype(F32)[0:1, :]
        second = qg_ref[2 * p + 1, 128:144, 0:128].astype(F32)[0:1, :]
        block = jnp.where(low, first, second)
        early.append(block * SPAN + row)
        late.append((127.0 - block) * SPAN + row)
    return jnp.concatenate(early, axis=1), jnp.concatenate(late, axis=1)


def key_positions(kv_ref, late):
    row = lax.broadcasted_iota(jnp.int32, (SPAN, 128), 0).astype(F32)
    out = []
    for j in range(NY):
        block = kv_ref[j, 256:272, 0:128].astype(F32)[0:1, :]
        base = (127.0 - block) * SPAN if late else block * SPAN
        out.append(base + row)
    column = jnp.concatenate(out, axis=0)
    return jnp.concatenate([column] * 4, axis=1)


def rows_of(ref, start, head):
    part = ref[:, start : start + SPAN, head * HEAD : (head + 1) * HEAD]
    return part.reshape(part.shape[0] * SPAN, HEAD)


def stats_kernel(qg_ref, kva_ref, kvb_ref, out_ref, s_ref, st_ref):
    q_early, q_late = query_positions(qg_ref)
    sides = (kva_ref, kvb_ref)
    for head in range(2):
        for part in range(2):
            q = rows_of(qg_ref, part * SPAN, head)
            top = None
            units = []
            for n, kv in enumerate(sides):
                units.append((n, kv, 0, part == 0))
                if part == 1:
                    units.append((n + 2, kv, SPAN, True))
            for slot, kv, start, masked in units:
                s = dot_nt(rows_of(kv, start, head), q) * SCALE
                if masked:
                    qp = q_late if start else q_early
                    s = jnp.where(key_positions(kv, start > 0) <= qp, s, MASKED)
                s_ref[slot] = s
                here = jnp.max(s.reshape(32, 8, 512), axis=0)
                top = here if top is None else jnp.maximum(top, here)
            top = jnp.max(top, axis=0, keepdims=True).astype(BF16).astype(F32)
            total = jnp.zeros((8, 512), F32)
            for slot, kv, start, masked in units:
                p = jnp.exp2(s_ref[slot] - top)
                total = total + jnp.sum(p.reshape(32, 8, 512), axis=0)
            total = jnp.sum(total, axis=0, keepdims=True)
            high = total.astype(BF16).astype(F32)
            low = total - high
            base = (head * 2 + part) * 12
            for r in range(4):
                lanes = slice(r * 128, (r + 1) * 128)
                st_ref[base + r : base + r + 1, :] = top[:, lanes]
                st_ref[base + 4 + r : base + 5 + r, :] = high[:, lanes]
                st_ref[base + 8 + r : base + 9 + r, :] = low[:, lanes]
    out_ref[...] = st_ref[...].astype(BF16)


def pack_kernel(acc_ref, recv_ref, lat_ref, proj_ref, o_ref, st_ref, out_ref, d_ref):
    coupled = acc_ref[...] + recv_ref[...]
    shifts = coupled[:, 0:64]
    log_scale = coupled[:, 64:128]
    damping = jnp.exp(-log_scale)
    normed = (lat_ref[...] - shifts) * damping
    upstream = jnp.concatenate([-normed * damping, 1.0 - normed * normed], axis=1).astype(BF16)
    d_ref[...] = jnp.zeros((16, 128), F32)
    for head in range(2):
        cols = slice(head * HEAD, (head + 1) * HEAD)
        grad = dot_nt(upstream, proj_ref[cols, :]).astype(BF16)
        product = grad.astype(F32) * o_ref[:, cols].astype(F32)
        delta = jnp.sum(product.T, axis=0, keepdims=True)
        high = delta.astype(BF16).astype(F32)
        d_ref[2 * head : 2 * head + 1, :] = high
        d_ref[2 * head + 1 : 2 * head + 2, :] = delta - high
    deltas = d_ref[...].astype(BF16)
    stats = st_ref[...]
    for i in range(NZ):
        out_ref[i, 0:128, :] = upstream
        out_ref[i, 128:144, :] = deltas
        out_ref[i, 144:192, :] = stats


def main_kernel(qg_ref, kva_ref, kvb_ref, g_ref, proj_ref, dq_ref, da_ref, db_ref, ds_ref):
    q_early, q_late = query_positions(qg_ref)
    lane = lax.broadcasted_iota(jnp.int32, (1, 128), 1)
    low = lane < SPAN
    upstream = [
        g_ref[:, part * SPAN : (part + 1) * SPAN, :].reshape(NZ * SPAN, HEAD) for part in range(2)
    ]
    tails = [g_ref[i, 128:144, :].astype(F32) for i in range(NZ)]
    turned = [pltpu.roll(t, SPAN, 1) for t in tails]
    stats = g_ref[:, 144:192, :].astype(F32)
    sides = (kva_ref, kvb_ref)
    grads = (da_ref, db_ref)
    for head in range(2):
        cols = slice(head * HEAD, (head + 1) * HEAD)
        proj = proj_ref[cols, :]
        lse, delta, q, dout = [], [], [], []
        for part in range(2):
            base = (head * 2 + part) * 12
            tops = stats[:, base : base + 4, :]
            sums = stats[:, base + 4 : base + 8, :] + stats[:, base + 8 : base + 12, :]
            top = jnp.max(tops, axis=0)
            total = jnp.sum(sums * jnp.exp2(tops - top[None]), axis=0)
            value = top + jnp.log(total) * LOG2E
            lse.append(jnp.concatenate([value[r : r + 1, :] for r in range(4)], axis=1))
            pieces = []
            for p in range(NZ // 2):
                left = (tails if part == 0 else turned)[2 * p]
                right = (turned if part == 0 else tails)[2 * p + 1]
                both = jnp.where(low, left, right)
                pieces.append(both[2 * head : 2 * head + 1, :] + both[2 * head + 1 : 2 * head + 2, :])
            delta.append(jnp.concatenate(pieces, axis=1))
            q.append(rows_of(qg_ref, part * SPAN, head))
            dout.append(dot_nt(upstream[part], proj).astype(BF16))

        def unit(keys, values, kp, part):
            t = dot_nt(keys, q[part]) * SCALE - lse[part]
            if kp is not None:
                t = jnp.where(kp <= (q_late if part else q_early), t, MASKED)
            p = jnp.exp2(t)
            ds = p * (dot_nt(values, dout[part]) - delta[part])
            return p.astype(BF16), ds.astype(BF16)

        for n in range(2):
            kv, grad = sides[n], grads[n]
            keys = rows_of(kv, 0, head)
            values = rows_of(kv, 128, head)
            pe, se = unit(keys, values, key_positions(kv, False), 0)
            ds_ref[n * 256 : (n + 1) * 256, 0:512] = se
            dv = dot(pe, dout[0])
            dk = dot(se, q[0])
            pd, sd = unit(keys, values, None, 1)
            ds_ref[n * 256 : (n + 1) * 256, 512:1024] = sd
            dv = dv + dot(pd, dout[1])
            dk = dk + dot(sd, q[1])
            grad[:, 0:64, cols] = (dk * FACTOR).astype(BF16).reshape(NY, SPAN, HEAD)
            grad[:, 128:192, cols] = dv.astype(BF16).reshape(NY, SPAN, HEAD)
            keys = rows_of(kv, 64, head)
            values = rows_of(kv, 192, head)
            pd, sd = unit(keys, values, key_positions(kv, True), 1)
            ds_ref[512 + n * 256 : 512 + (n + 1) * 256, 512:1024] = sd
            dv = dot(pd, dout[1])
            dk = dot(sd, q[1])
            grad[:, 64:128, cols] = (dk * FACTOR).astype(BF16).reshape(NY, SPAN, HEAD)
            grad[:, 192:256, cols] = dv.astype(BF16).reshape(NY, SPAN, HEAD)
        early_t = jnp.concatenate([rows_of(kv, 0, head) for kv in sides], axis=0).T
        late_t = jnp.concatenate([rows_of(kv, 64, head) for kv in sides], axis=0).T
        dqe = dot(early_t, ds_ref[0:512, 0:512])
        dql = dot(early_t, ds_ref[0:512, 512:1024]) + dot(late_t, ds_ref[512:1024, 512:1024])
        dq_ref[:, 0:64, cols] = (dqe * FACTOR).T.astype(BF16).reshape(NZ, SPAN, HEAD)
        dq_ref[:, 64:128, cols] = (dql * FACTOR).T.astype(BF16).reshape(NZ, SPAN, HEAD)


def fold_kernel(own_ref, recv_ref, o0_ref, o1_ref, o2_ref, o3_ref):
    o0_ref[...] = own_ref[0].astype(F32) + recv_ref[0].astype(F32)
    for k, ref in ((1, o1_ref), (2, o2_ref), (3, o3_ref)):
        ref[...] = (own_ref[k].astype(F32) + recv_ref[k].astype(F32)).astype(BF16)


def final_kernel(own_ref, r1_ref, r2_ref, r3_ref, dq_ref, qo_ref, ko_ref, vo_ref):
    total = own_ref[...]
    for ref in (r1_ref, r2_ref, r3_ref):
        total = total + ref[...].astype(F32)
    ko_ref[...] = total[0:128, :].astype(BF16)
    vo_ref[...] = total[128:256, :].astype(BF16)
    dq = dq_ref[0].astype(F32)
    for i in range(1, NZ):
        dq = dq + dq_ref[i].astype(F32)
    qo_ref[...] = dq.astype(BF16)


def call(kernel, outs, cost, scratch=(), smem=0, limit=48):
    vmem = pl.BlockSpec(memory_space=pltpu.VMEM)

    def run(*args):
        specs = [vmem] * len(args)
        if smem:
            specs[0] = pl.BlockSpec(memory_space=pltpu.SMEM)
        return pl.pallas_call(
            kernel,
            out_shape=[jax.ShapeDtypeStruct(s, d) for s, d in outs],
            in_specs=specs,
            out_specs=[vmem] * len(outs),
            scratch_shapes=list(scratch),
            compiler_params=pltpu.CompilerParams(vmem_limit_bytes=limit * MIB),
            cost_estimate=pl.CostEstimate(flops=cost, bytes_accessed=2 * MIB, transcendentals=0),
        )(*args)

    return run


def swap(x, axis, size, k):
    return lax.ppermute(x, axis, [(i, i ^ k) for i in range(size)])


def local(n_tp, latent, positions, queries, keys, values, attention_out, projection):
    with jax.named_scope("prep"):
        qpay, kvpay, total = call(
            prep_kernel,
            [((NZ, 144, 256), BF16), ((272, 256), BF16), ((128, 128), F32)],
            10_000_000,
            smem=1,
        )(positions, queries, keys, values, attention_out, projection)
    with jax.named_scope("kv_over_y"):
        arrived = [swap(kvpay, "y", NY, k) for k in (1, 2, 3)]
    rounds = [k for k in (2, 4, 1) if k < n_tp]
    extra = jnp.zeros_like(total)
    for n, k in enumerate(rounds):
        with jax.named_scope("coupled_over_tp"):
            extra = swap(total, "tp", n_tp, k)
            if n < len(rounds) - 1:
                total = total + extra
    with jax.named_scope("q_over_z"):
        qg = lax.all_to_all(qpay, "z", 0, 0)
    with jax.named_scope("kv_over_core"):
        kva = jnp.stack([kvpay] + arrived)
        kvb = swap(kva, "c", NC, 1)
    with jax.named_scope("stats"):
        (stats,) = call(
            stats_kernel,
            [((48, 128), BF16)],
            1_000_000_000,
            [pltpu.VMEM((4, 256, 512), F32), pltpu.VMEM((48, 128), F32)],
        )(qg, kva, kvb)
    with jax.named_scope("pack"):
        (pay,) = call(
            pack_kernel, [((NZ, 192, 128), BF16)], 10_000_000, [pltpu.VMEM((16, 128), F32)]
        )(total, extra, latent, projection, attention_out, stats)
    with jax.named_scope("upstream_over_z"):
        gathered = lax.all_to_all(pay, "z", 0, 0)
    with jax.named_scope("main"):
        dq, da, db = call(
            main_kernel,
            [((NZ, 128, 256), BF16), ((NY, 256, 256), BF16), ((NY, 256, 256), BF16)],
            4_000_000_000,
            [pltpu.VMEM((1024, 1024), BF16)],
        )(qg, kva, kvb, gathered, projection)
    with jax.named_scope("dkv_over_core"):
        other = swap(db, "c", NC, 1)
        own, *send = call(fold_kernel, [((256, 256), F32)] + [((256, 256), BF16)] * 3, 1_000_000)(
            da, other
        )
    with jax.named_scope("dkv_over_y"):
        back = [swap(s, "y", NY, k) for k, s in zip((1, 2, 3), send)]
    with jax.named_scope("dq_over_z"):
        dqs = lax.all_to_all(dq, "z", 0, 0)
    with jax.named_scope("final"):
        return tuple(
            call(final_kernel, [((128, 256), BF16)] * 3, 1_000_000)(own, *back, dqs)
        )


def solution(mesh):
    n_tp = mesh.shape["tp"]
    fine = Mesh(mesh.devices.reshape(NY, NZ, NC, n_tp), ("y", "z", "c", "tp"))
    ctx = ("y", "z", "c")
    placed = (
        P(ctx, None),
        P(ctx),
        P(ctx, "tp"),
        P(ctx, "tp"),
        P(ctx, "tp"),
        P(ctx, "tp"),
        P("tp", None),
    )
    return jax.shard_map(
        functools.partial(local, n_tp),
        mesh=fine,
        in_specs=placed,
        out_specs=(P(ctx, "tp"), P(ctx, "tp"), P(ctx, "tp")),
        check_vma=False,
    )
```

```python
import functools

import jax
import jax.numpy as jnp
from jax import lax
from jax.experimental import pallas as pl
from jax.experimental.pallas import tpu as pltpu
from jax.sharding import Mesh, PartitionSpec as P

HEAD = 128
SPAN = 64
NZ, NY, NC = 8, 4, 2
LOG2E = 1.4426950408889634
FACTOR = HEAD ** (-0.5)
SCALE = FACTOR * LOG2E
MASKED = -(2.0**100)
F32 = jnp.float32
BF16 = jnp.bfloat16
NT = (((1,), (1,)), ((), ()))
MIB = 1 << 20
JOIN_COST = 1_000_000
FOLD_COST = 20_000_000_000


def dot_nt(a, b):
    return lax.dot_general(a, b, NT, preferred_element_type=F32)


def dot(a, b):
    return jnp.dot(a, b, preferred_element_type=F32)


def prep_kernel(
    pos_ref, q_hbm, k_hbm, v_hbm, o_hbm, proj_hbm, qpay_ref, kvpay_ref, part_ref, *scratch
):
    buffers, sems = scratch[:-1], scratch[-1]
    sources = (k_hbm, v_hbm, q_hbm, o_hbm, proj_hbm)
    copies = [
        pltpu.make_async_copy(src, dst, sems.at[n])
        for n, (src, dst) in enumerate(zip(sources, buffers))
    ]
    for copy in copies:
        copy.start()
    k_ref, v_ref, q_ref, o_ref, proj_ref = buffers
    block = lax.shift_right_logical(pos_ref[0], 6).astype(F32)
    tag = jnp.full((16, 256), block, F32).astype(BF16)
    for copy in copies:
        copy.wait()
    k, v, q = k_ref[...], v_ref[...], q_ref[...]
    kvpay_ref[0:128, :] = k
    kvpay_ref[128:256, :] = v
    kvpay_ref[256:272, :] = tag
    for i in range(NZ):
        qpay_ref[i, 0:128, :] = q
        qpay_ref[i, 128:144, :] = tag
    part_ref[...] = dot(o_ref[...], proj_ref[...])


def query_positions(qg_ref):
    lane = lax.broadcasted_iota(jnp.int32, (1, 128), 1)
    low = lane < SPAN
    row = (lane & (SPAN - 1)).astype(F32)
    early, late = [], []
    for p in range(NZ // 2):
        first = qg_ref[2 * p, 128:144, 0:128].astype(F32)[0:1, :]
        second = qg_ref[2 * p + 1, 128:144, 0:128].astype(F32)[0:1, :]
        block = jnp.where(low, first, second)
        early.append(block * SPAN + row)
        late.append((127.0 - block) * SPAN + row)
    return jnp.concatenate(early, axis=1), jnp.concatenate(late, axis=1)


def key_positions(kv_ref, late):
    row = lax.broadcasted_iota(jnp.int32, (SPAN, 128), 0).astype(F32)
    out = []
    for j in range(NY):
        block = kv_ref[j, 256:272, 0:128].astype(F32)[0:1, :]
        base = (127.0 - block) * SPAN if late else block * SPAN
        out.append(base + row)
    column = jnp.concatenate(out, axis=0)
    return jnp.concatenate([column] * 4, axis=1)


def rows_of(ref, start, head):
    part = ref[:, start : start + SPAN, head * HEAD : (head + 1) * HEAD]
    return part.reshape(part.shape[0] * SPAN, HEAD)


def stats_kernel(qg_ref, kva_ref, kvb_ref, out_ref, s_ref, st_ref):
    q_early, q_late = query_positions(qg_ref)
    sides = (kva_ref, kvb_ref)
    for head in range(2):
        for part in range(2):
            q = rows_of(qg_ref, part * SPAN, head)
            top = None
            units = []
            for n, kv in enumerate(sides):
                units.append((n, kv, 0, part == 0))
                if part == 1:
                    units.append((n + 2, kv, SPAN, True))
            for slot, kv, start, masked in units:
                s = dot_nt(rows_of(kv, start, head), q) * SCALE
                if masked:
                    qp = q_late if start else q_early
                    s = jnp.where(key_positions(kv, start > 0) <= qp, s, MASKED)
                s_ref[slot] = s
                here = jnp.max(s.reshape(32, 8, 512), axis=0)
                top = here if top is None else jnp.maximum(top, here)
            top = jnp.max(top, axis=0, keepdims=True).astype(BF16).astype(F32)
            total = jnp.zeros((8, 512), F32)
            for slot, kv, start, masked in units:
                p = jnp.exp2(s_ref[slot] - top)
                total = total + jnp.sum(p.reshape(32, 8, 512), axis=0)
            total = jnp.sum(total, axis=0, keepdims=True)
            high = total.astype(BF16).astype(F32)
            low = total - high
            base = (head * 2 + part) * 12
            for r in range(4):
                lanes = slice(r * 128, (r + 1) * 128)
                st_ref[base + r : base + r + 1, :] = top[:, lanes]
                st_ref[base + 4 + r : base + 5 + r, :] = high[:, lanes]
                st_ref[base + 8 + r : base + 9 + r, :] = low[:, lanes]
    out_ref[...] = st_ref[...].astype(BF16)


def join_kernel(own_ref, r1_ref, r2_ref, r3_ref, total_ref, recv_ref, kv_ref, sum_ref):
    for n, ref in enumerate((own_ref, r1_ref, r2_ref, r3_ref)):
        kv_ref[n] = ref[...]
    sum_ref[...] = total_ref[...] + recv_ref[...]


def pack_kernel(total_ref, recv_ref, lat_ref, proj_ref, o_ref, st_ref, out_ref, d_ref):
    coupled = total_ref[...] + recv_ref[...]
    shifts = coupled[:, 0:64]
    log_scale = coupled[:, 64:128]
    damping = jnp.exp(-log_scale)
    normed = (lat_ref[...].T - shifts) * damping
    upstream = jnp.concatenate([-normed * damping, 1.0 - normed * normed], axis=1).astype(BF16)
    d_ref[...] = jnp.zeros((16, 128), F32)
    for head in range(2):
        cols = slice(head * HEAD, (head + 1) * HEAD)
        grad = dot_nt(upstream, proj_ref[cols, :]).astype(BF16)
        product = grad.astype(F32) * o_ref[:, cols].astype(F32)
        delta = jnp.sum(product.T, axis=0, keepdims=True)
        high = delta.astype(BF16).astype(F32)
        d_ref[2 * head : 2 * head + 1, :] = high
        d_ref[2 * head + 1 : 2 * head + 2, :] = delta - high
    deltas = d_ref[...].astype(BF16)
    stats = st_ref[...]
    for i in range(NZ):
        out_ref[i, 0:128, :] = upstream
        out_ref[i, 128:144, :] = deltas
        out_ref[i, 144:192, :] = stats


def main_kernel(qg_ref, kva_ref, kvb_ref, g_ref, proj_ref, dq_ref, da_ref, db_ref, ds_ref):
    q_early, q_late = query_positions(qg_ref)
    lane = lax.broadcasted_iota(jnp.int32, (1, 128), 1)
    low = lane < SPAN
    upstream = [
        g_ref[:, part * SPAN : (part + 1) * SPAN, :].reshape(NZ * SPAN, HEAD) for part in range(2)
    ]
    tails = [g_ref[i, 128:144, :].astype(F32) for i in range(NZ)]
    turned = [pltpu.roll(t, SPAN, 1) for t in tails]
    stats = g_ref[:, 144:192, :].astype(F32)
    sides = (kva_ref, kvb_ref)
    grads = (da_ref, db_ref)
    for head in range(2):
        cols = slice(head * HEAD, (head + 1) * HEAD)
        proj = proj_ref[cols, :]
        lse, delta, q, dout = [], [], [], []
        for part in range(2):
            base = (head * 2 + part) * 12
            tops = stats[:, base : base + 4, :]
            sums = stats[:, base + 4 : base + 8, :] + stats[:, base + 8 : base + 12, :]
            top = jnp.max(tops, axis=0)
            total = jnp.sum(sums * jnp.exp2(tops - top[None]), axis=0)
            value = top + jnp.log(total) * LOG2E
            lse.append(jnp.concatenate([value[r : r + 1, :] for r in range(4)], axis=1))
            pieces = []
            for p in range(NZ // 2):
                left = (tails if part == 0 else turned)[2 * p]
                right = (turned if part == 0 else tails)[2 * p + 1]
                both = jnp.where(low, left, right)
                pieces.append(both[2 * head : 2 * head + 1, :] + both[2 * head + 1 : 2 * head + 2, :])
            delta.append(jnp.concatenate(pieces, axis=1))
            q.append(rows_of(qg_ref, part * SPAN, head))
            dout.append(dot_nt(upstream[part], proj).astype(BF16))

        def unit(keys, values, kp, part):
            t = dot_nt(keys, q[part]) * SCALE - lse[part]
            if kp is not None:
                t = jnp.where(kp <= (q_late if part else q_early), t, MASKED)
            p = jnp.exp2(t)
            ds = p * (dot_nt(values, dout[part]) - delta[part])
            return p.astype(BF16), ds.astype(BF16)

        for n in range(2):
            kv, grad = sides[n], grads[n]
            keys = rows_of(kv, 0, head)
            values = rows_of(kv, 128, head)
            pe, se = unit(keys, values, key_positions(kv, False), 0)
            ds_ref[n * 256 : (n + 1) * 256, 0:512] = se
            dv = dot(pe, dout[0])
            dk = dot(se, q[0])
            pd, sd = unit(keys, values, None, 1)
            ds_ref[n * 256 : (n + 1) * 256, 512:1024] = sd
            dv = dv + dot(pd, dout[1])
            dk = dk + dot(sd, q[1])
            grad[:, 0:64, cols] = (dk * FACTOR).astype(BF16).reshape(NY, SPAN, HEAD)
            grad[:, 128:192, cols] = dv.astype(BF16).reshape(NY, SPAN, HEAD)
            keys = rows_of(kv, 64, head)
            values = rows_of(kv, 192, head)
            pd, sd = unit(keys, values, key_positions(kv, True), 1)
            ds_ref[512 + n * 256 : 512 + (n + 1) * 256, 512:1024] = sd
            dv = dot(pd, dout[1])
            dk = dot(sd, q[1])
            grad[:, 64:128, cols] = (dk * FACTOR).astype(BF16).reshape(NY, SPAN, HEAD)
            grad[:, 192:256, cols] = dv.astype(BF16).reshape(NY, SPAN, HEAD)
        early_t = jnp.concatenate([rows_of(kv, 0, head) for kv in sides], axis=0).T
        late_t = jnp.concatenate([rows_of(kv, 64, head) for kv in sides], axis=0).T
        dqe = dot(early_t, ds_ref[0:512, 0:512])
        dql = dot(early_t, ds_ref[0:512, 512:1024]) + dot(late_t, ds_ref[512:1024, 512:1024])
        dq_ref[:, 0:64, cols] = (dqe * FACTOR).T.astype(BF16).reshape(NZ, SPAN, HEAD)
        dq_ref[:, 64:128, cols] = (dql * FACTOR).T.astype(BF16).reshape(NZ, SPAN, HEAD)


def fold_kernel(own_ref, recv_ref, o0_ref, o1_ref, o2_ref, o3_ref):
    o0_ref[...] = own_ref[0].astype(F32) + recv_ref[0].astype(F32)
    for k, ref in ((1, o1_ref), (2, o2_ref), (3, o3_ref)):
        ref[...] = (own_ref[k].astype(F32) + recv_ref[k].astype(F32)).astype(BF16)


def final_kernel(own_ref, r1_ref, r2_ref, r3_ref, dq_ref, qo_ref, ko_ref, vo_ref):
    total = own_ref[...]
    for ref in (r1_ref, r2_ref, r3_ref):
        total = total + ref[...].astype(F32)
    ko_ref[...] = total[0:128, :].astype(BF16)
    vo_ref[...] = total[128:256, :].astype(BF16)
    dq = dq_ref[0].astype(F32)
    for i in range(1, NZ):
        dq = dq + dq_ref[i].astype(F32)
    qo_ref[...] = dq.astype(BF16)


def call(kernel, outs, cost, scratch=(), specs=None, limit=48):
    vmem = pl.BlockSpec(memory_space=pltpu.VMEM)

    def run(*args):
        return pl.pallas_call(
            kernel,
            out_shape=[jax.ShapeDtypeStruct(s, d) for s, d in outs],
            in_specs=specs or [vmem] * len(args),
            out_specs=[vmem] * len(outs),
            scratch_shapes=list(scratch),
            compiler_params=pltpu.CompilerParams(vmem_limit_bytes=limit * MIB),
            cost_estimate=pl.CostEstimate(flops=cost, bytes_accessed=2 * MIB, transcendentals=0),
        )(*args)

    return run


def swap(x, axis, size, k):
    return lax.ppermute(x, axis, [(i, i ^ k) for i in range(size)])


def local(n_x, n_h, latent, positions, queries, keys, values, attention_out, projection):
    with jax.named_scope("prep"):
        qpay, kvpay, total = call(
            prep_kernel,
            [((NZ, 144, 256), BF16), ((272, 256), BF16), ((128, 128), F32)],
            10_000_000,
            [pltpu.VMEM((128, 256), BF16)] * 4
            + [pltpu.VMEM((256, 128), BF16), pltpu.SemaphoreType.DMA((5,))],
            [pl.BlockSpec(memory_space=pltpu.SMEM)] + [pl.BlockSpec(memory_space=pltpu.HBM)] * 5,
            limit=62,
        )(positions, queries, keys, values, attention_out, projection)
    with jax.named_scope("kv_over_y"):
        arrived = [swap(kvpay, "y", NY, k) for k in (1, 2, 3)]
    with jax.named_scope("coupled_over_h"):
        total = total + swap(total, "h", n_h, 1) if n_h > 1 else total
    with jax.named_scope("coupled_over_x"):
        first = swap(total, "x", n_x, 1) if n_x > 1 else jnp.zeros_like(total)
    with jax.named_scope("q_over_z"):
        qg = lax.all_to_all(qpay, "z", 0, 0)
    with jax.named_scope("join"):
        kva, total = call(
            join_kernel, [((NY, 272, 256), BF16), ((128, 128), F32)], JOIN_COST
        )(kvpay, *arrived, total, first)
    with jax.named_scope("coupled_over_x"):
        second = swap(total, "x", n_x, 2) if n_x > 1 else jnp.zeros_like(total)
    with jax.named_scope("kv_over_core"):
        kvb = swap(kva, "c", NC, 1)
    with jax.named_scope("stats"):
        (stats,) = call(
            stats_kernel,
            [((48, 128), BF16)],
            1_000_000_000,
            [pltpu.VMEM((4, 256, 512), F32), pltpu.VMEM((48, 128), F32)],
        )(qg, kva, kvb)
    with jax.named_scope("pack"):
        (pay,) = call(
            pack_kernel, [((NZ, 192, 128), BF16)], 10_000_000, [pltpu.VMEM((16, 128), F32)]
        )(total, second, latent.T, projection, attention_out, stats)
    with jax.named_scope("upstream_over_z"):
        gathered = lax.all_to_all(pay, "z", 0, 0)
    with jax.named_scope("main"):
        dq, da, db = call(
            main_kernel,
            [((NZ, 128, 256), BF16), ((NY, 256, 256), BF16), ((NY, 256, 256), BF16)],
            4_000_000_000,
            [pltpu.VMEM((1024, 1024), BF16)],
        )(qg, kva, kvb, gathered, projection)
    with jax.named_scope("dkv_over_core"):
        other = swap(db, "c", NC, 1)
        own, *send = call(
            fold_kernel, [((256, 256), F32)] + [((256, 256), BF16)] * 3, FOLD_COST
        )(da, other)
    with jax.named_scope("dkv_over_y"):
        back = [swap(s, "y", NY, k) for k, s in zip((1, 2, 3), send)]
    with jax.named_scope("dq_over_z"):
        dqs = lax.all_to_all(dq, "z", 0, 0)
    with jax.named_scope("final"):
        return tuple(
            call(final_kernel, [((128, 256), BF16)] * 3, 1_000_000)(own, *back, dqs)
        )


def solution(mesh):
    n_h = min(2, mesh.shape["tp"])
    n_x = mesh.shape["tp"] // n_h
    fine = Mesh(mesh.devices.reshape(NY, NZ, NC, n_x, n_h), ("y", "z", "c", "x", "h"))
    ctx = ("y", "z", "c")
    tp = ("x", "h")
    placed = (
        P(ctx, None),
        P(ctx),
        P(ctx, tp),
        P(ctx, tp),
        P(ctx, tp),
        P(ctx, tp),
        P(tp, None),
    )
    return jax.shard_map(
        functools.partial(local, n_x, n_h),
        mesh=fine,
        in_specs=placed,
        out_specs=(P(ctx, tp), P(ctx, tp), P(ctx, tp)),
        check_vma=False,
    )
```

```python
import functools

import jax
import jax.numpy as jnp
from jax import lax
from jax.experimental import pallas as pl
from jax.experimental.pallas import tpu as pltpu
from jax.sharding import Mesh, PartitionSpec as P

HEAD = 128
SPAN = 64
NZ, NY, NC = 8, 4, 2
LOG2E = 1.4426950408889634
FACTOR = HEAD ** (-0.5)
SCALE = FACTOR * LOG2E
MASKED = -(2.0**100)
F32 = jnp.float32
BF16 = jnp.bfloat16
NT = (((1,), (1,)), ((), ()))
MIB = 1 << 20
JOIN_COST = 20_000_000_000
FOLD_COST = 20_000_000_000


def dot_nt(a, b):
    return lax.dot_general(a, b, NT, preferred_element_type=F32)


def dot(a, b):
    return jnp.dot(a, b, preferred_element_type=F32)


def prep_kernel(
    pos_ref, q_hbm, k_hbm, v_hbm, o_hbm, proj_hbm, qpay_ref, kvpay_ref, part_ref, *scratch
):
    buffers, sems = scratch[:-1], scratch[-1]
    sources = (k_hbm, v_hbm, q_hbm, o_hbm, proj_hbm)
    copies = [
        pltpu.make_async_copy(src, dst, sems.at[n])
        for n, (src, dst) in enumerate(zip(sources, buffers))
    ]
    for copy in copies:
        copy.start()
    k_ref, v_ref, q_ref, o_ref, proj_ref = buffers
    block = lax.shift_right_logical(pos_ref[0], 6).astype(F32)
    tag = jnp.full((16, 256), block, F32).astype(BF16)
    for copy in copies:
        copy.wait()
    k, v, q = k_ref[...], v_ref[...], q_ref[...]
    kvpay_ref[0:128, :] = k
    kvpay_ref[128:256, :] = v
    kvpay_ref[256:272, :] = tag
    for i in range(NZ):
        qpay_ref[i, 0:128, :] = q
        qpay_ref[i, 128:144, :] = tag
    part_ref[...] = dot(o_ref[...], proj_ref[...])


def query_positions(qg_ref):
    lane = lax.broadcasted_iota(jnp.int32, (1, 128), 1)
    low = lane < SPAN
    row = (lane & (SPAN - 1)).astype(F32)
    early, late = [], []
    for p in range(NZ // 2):
        first = qg_ref[2 * p, 128:144, 0:128].astype(F32)[0:1, :]
        second = qg_ref[2 * p + 1, 128:144, 0:128].astype(F32)[0:1, :]
        block = jnp.where(low, first, second)
        early.append(block * SPAN + row)
        late.append((127.0 - block) * SPAN + row)
    return jnp.concatenate(early, axis=1), jnp.concatenate(late, axis=1)


def key_positions(kv_ref, late):
    row = lax.broadcasted_iota(jnp.int32, (SPAN, 128), 0).astype(F32)
    out = []
    for j in range(NY):
        block = kv_ref[j, 256:272, 0:128].astype(F32)[0:1, :]
        base = (127.0 - block) * SPAN if late else block * SPAN
        out.append(base + row)
    column = jnp.concatenate(out, axis=0)
    return jnp.concatenate([column] * 4, axis=1)


def rows_of(ref, start, head):
    part = ref[:, start : start + SPAN, head * HEAD : (head + 1) * HEAD]
    return part.reshape(part.shape[0] * SPAN, HEAD)


def stats_kernel(qg_ref, kva_ref, kvb_ref, out_ref, s_ref, st_ref):
    q_early, q_late = query_positions(qg_ref)
    sides = (kva_ref, kvb_ref)
    for head in range(2):
        for part in range(2):
            q = rows_of(qg_ref, part * SPAN, head)
            top = None
            units = []
            for n, kv in enumerate(sides):
                units.append((n, kv, 0, part == 0))
                if part == 1:
                    units.append((n + 2, kv, SPAN, True))
            for slot, kv, start, masked in units:
                s = dot_nt(rows_of(kv, start, head), q) * SCALE
                if masked:
                    qp = q_late if start else q_early
                    s = jnp.where(key_positions(kv, start > 0) <= qp, s, MASKED)
                s_ref[slot] = s
                here = jnp.max(s.reshape(32, 8, 512), axis=0)
                top = here if top is None else jnp.maximum(top, here)
            top = jnp.max(top, axis=0, keepdims=True).astype(BF16).astype(F32)
            total = jnp.zeros((8, 512), F32)
            for slot, kv, start, masked in units:
                p = jnp.exp2(s_ref[slot] - top)
                total = total + jnp.sum(p.reshape(32, 8, 512), axis=0)
            total = jnp.sum(total, axis=0, keepdims=True)
            high = total.astype(BF16).astype(F32)
            low = total - high
            base = (head * 2 + part) * 12
            for r in range(4):
                lanes = slice(r * 128, (r + 1) * 128)
                st_ref[base + r : base + r + 1, :] = top[:, lanes]
                st_ref[base + 4 + r : base + 5 + r, :] = high[:, lanes]
                st_ref[base + 8 + r : base + 9 + r, :] = low[:, lanes]
    out_ref[...] = st_ref[...].astype(BF16)


def join_kernel(own_ref, r1_ref, r2_ref, r3_ref, kv_ref):
    for n, ref in enumerate((own_ref, r1_ref, r2_ref, r3_ref)):
        kv_ref[n] = ref[...]


def spread_kernel(part_ref, *refs):
    out_ref = refs[-1]
    part = part_ref[...]
    for n in range(out_ref.shape[0]):
        out_ref[n] = part


def pack_kernel(parts_ref, lat_ref, proj_ref, o_ref, st_ref, out_ref, d_ref):
    coupled = parts_ref[0]
    for n in range(1, parts_ref.shape[0]):
        coupled = coupled + parts_ref[n]
    shifts = coupled[:, 0:64]
    log_scale = coupled[:, 64:128]
    damping = jnp.exp(-log_scale)
    normed = (lat_ref[...].T - shifts) * damping
    upstream = jnp.concatenate([-normed * damping, 1.0 - normed * normed], axis=1).astype(BF16)
    d_ref[...] = jnp.zeros((16, 128), F32)
    for head in range(2):
        cols = slice(head * HEAD, (head + 1) * HEAD)
        grad = dot_nt(upstream, proj_ref[cols, :]).astype(BF16)
        product = grad.astype(F32) * o_ref[:, cols].astype(F32)
        delta = jnp.sum(product.T, axis=0, keepdims=True)
        high = delta.astype(BF16).astype(F32)
        d_ref[2 * head : 2 * head + 1, :] = high
        d_ref[2 * head + 1 : 2 * head + 2, :] = delta - high
    deltas = d_ref[...].astype(BF16)
    stats = st_ref[...]
    for i in range(NZ):
        out_ref[i, 0:128, :] = upstream
        out_ref[i, 128:144, :] = deltas
        out_ref[i, 144:192, :] = stats


def main_kernel(qg_ref, kva_ref, kvb_ref, g_ref, proj_ref, dq_ref, da_ref, db_ref, ds_ref):
    q_early, q_late = query_positions(qg_ref)
    lane = lax.broadcasted_iota(jnp.int32, (1, 128), 1)
    low = lane < SPAN
    upstream = [
        g_ref[:, part * SPAN : (part + 1) * SPAN, :].reshape(NZ * SPAN, HEAD) for part in range(2)
    ]
    tails = [g_ref[i, 128:144, :].astype(F32) for i in range(NZ)]
    turned = [pltpu.roll(t, SPAN, 1) for t in tails]
    stats = g_ref[:, 144:192, :].astype(F32)
    sides = (kva_ref, kvb_ref)
    grads = (da_ref, db_ref)
    for head in range(2):
        cols = slice(head * HEAD, (head + 1) * HEAD)
        proj = proj_ref[cols, :]
        lse, delta, q, dout = [], [], [], []
        for part in range(2):
            base = (head * 2 + part) * 12
            tops = stats[:, base : base + 4, :]
            sums = stats[:, base + 4 : base + 8, :] + stats[:, base + 8 : base + 12, :]
            top = jnp.max(tops, axis=0)
            total = jnp.sum(sums * jnp.exp2(tops - top[None]), axis=0)
            value = top + jnp.log(total) * LOG2E
            lse.append(jnp.concatenate([value[r : r + 1, :] for r in range(4)], axis=1))
            pieces = []
            for p in range(NZ // 2):
                left = (tails if part == 0 else turned)[2 * p]
                right = (turned if part == 0 else tails)[2 * p + 1]
                both = jnp.where(low, left, right)
                pieces.append(both[2 * head : 2 * head + 1, :] + both[2 * head + 1 : 2 * head + 2, :])
            delta.append(jnp.concatenate(pieces, axis=1))
            q.append(rows_of(qg_ref, part * SPAN, head))
            dout.append(dot_nt(upstream[part], proj).astype(BF16))

        def unit(keys, values, kp, part):
            t = dot_nt(keys, q[part]) * SCALE - lse[part]
            if kp is not None:
                t = jnp.where(kp <= (q_late if part else q_early), t, MASKED)
            p = jnp.exp2(t)
            ds = p * (dot_nt(values, dout[part]) - delta[part])
            return p.astype(BF16), ds.astype(BF16)

        for n in range(2):
            kv, grad = sides[n], grads[n]
            keys = rows_of(kv, 0, head)
            values = rows_of(kv, 128, head)
            pe, se = unit(keys, values, key_positions(kv, False), 0)
            ds_ref[n * 256 : (n + 1) * 256, 0:512] = se
            dv = dot(pe, dout[0])
            dk = dot(se, q[0])
            pd, sd = unit(keys, values, None, 1)
            ds_ref[n * 256 : (n + 1) * 256, 512:1024] = sd
            dv = dv + dot(pd, dout[1])
            dk = dk + dot(sd, q[1])
            grad[:, 0:64, cols] = (dk * FACTOR).astype(BF16).reshape(NY, SPAN, HEAD)
            grad[:, 128:192, cols] = dv.astype(BF16).reshape(NY, SPAN, HEAD)
            keys = rows_of(kv, 64, head)
            values = rows_of(kv, 192, head)
            pd, sd = unit(keys, values, key_positions(kv, True), 1)
            ds_ref[512 + n * 256 : 512 + (n + 1) * 256, 512:1024] = sd
            dv = dot(pd, dout[1])
            dk = dot(sd, q[1])
            grad[:, 64:128, cols] = (dk * FACTOR).astype(BF16).reshape(NY, SPAN, HEAD)
            grad[:, 192:256, cols] = dv.astype(BF16).reshape(NY, SPAN, HEAD)
        early_t = jnp.concatenate([rows_of(kv, 0, head) for kv in sides], axis=0).T
        late_t = jnp.concatenate([rows_of(kv, 64, head) for kv in sides], axis=0).T
        dqe = dot(early_t, ds_ref[0:512, 0:512])
        dql = dot(early_t, ds_ref[0:512, 512:1024]) + dot(late_t, ds_ref[512:1024, 512:1024])
        dq_ref[:, 0:64, cols] = (dqe * FACTOR).T.astype(BF16).reshape(NZ, SPAN, HEAD)
        dq_ref[:, 64:128, cols] = (dql * FACTOR).T.astype(BF16).reshape(NZ, SPAN, HEAD)


def fold_kernel(own_ref, recv_ref, o0_ref, o1_ref, o2_ref, o3_ref):
    o0_ref[...] = own_ref[0].astype(F32) + recv_ref[0].astype(F32)
    for k, ref in ((1, o1_ref), (2, o2_ref), (3, o3_ref)):
        ref[...] = (own_ref[k].astype(F32) + recv_ref[k].astype(F32)).astype(BF16)


def final_kernel(own_ref, r1_ref, r2_ref, r3_ref, dq_ref, qo_ref, ko_ref, vo_ref):
    total = own_ref[...]
    for ref in (r1_ref, r2_ref, r3_ref):
        total = total + ref[...].astype(F32)
    ko_ref[...] = total[0:128, :].astype(BF16)
    vo_ref[...] = total[128:256, :].astype(BF16)
    dq = dq_ref[0].astype(F32)
    for i in range(1, NZ):
        dq = dq + dq_ref[i].astype(F32)
    qo_ref[...] = dq.astype(BF16)


def call(kernel, outs, cost, scratch=(), specs=None, limit=48):
    vmem = pl.BlockSpec(memory_space=pltpu.VMEM)

    def run(*args):
        return pl.pallas_call(
            kernel,
            out_shape=[jax.ShapeDtypeStruct(s, d) for s, d in outs],
            in_specs=specs or [vmem] * len(args),
            out_specs=[vmem] * len(outs),
            scratch_shapes=list(scratch),
            compiler_params=pltpu.CompilerParams(vmem_limit_bytes=limit * MIB),
            cost_estimate=pl.CostEstimate(flops=cost, bytes_accessed=2 * MIB, transcendentals=0),
        )(*args)

    return run


def swap(x, axis, size, k):
    return lax.ppermute(x, axis, [(i, i ^ k) for i in range(size)])


def local(n_tp, latent, positions, queries, keys, values, attention_out, projection):
    vmem, hbm, anywhere = (
        pl.BlockSpec(memory_space=m) for m in (pltpu.VMEM, pltpu.HBM, pl.ANY)
    )
    with jax.named_scope("prep"):
        qpay, kvpay, part = call(
            prep_kernel,
            [((NZ, 144, 256), BF16), ((272, 256), BF16), ((128, 128), F32)],
            10_000_000,
            [pltpu.VMEM((128, 256), BF16)] * 4
            + [pltpu.VMEM((256, 128), BF16), pltpu.SemaphoreType.DMA((5,))],
            [pl.BlockSpec(memory_space=pltpu.SMEM)] + [hbm] * 5,
            limit=62,
        )(positions, queries, keys, values, attention_out, projection)
    with jax.named_scope("kv_over_y"):
        arrived = [swap(kvpay, "y", NY, k) for k in (1, 2, 3)]
    with jax.named_scope("q_over_z"):
        qg = lax.all_to_all(qpay, "z", 0, 0)
    with jax.named_scope("coupled_over_tp"):
        (spread,) = call(
            spread_kernel, [((n_tp, 128, 128), F32)], 1_000_000, specs=[vmem, anywhere]
        )(part, qg)
        parts = lax.all_to_all(spread, ("x", "h"), 0, 0)
    with jax.named_scope("join"):
        (kva,) = call(join_kernel, [((NY, 272, 256), BF16)], JOIN_COST)(kvpay, *arrived)
    with jax.named_scope("kv_over_core"):
        kvb = swap(kva, "c", NC, 1)
    with jax.named_scope("stats"):
        (stats,) = call(
            stats_kernel,
            [((48, 128), BF16)],
            1_000_000_000,
            [pltpu.VMEM((4, 256, 512), F32), pltpu.VMEM((48, 128), F32)],
        )(qg, kva, kvb)
    with jax.named_scope("pack"):
        (pay,) = call(
            pack_kernel, [((NZ, 192, 128), BF16)], 10_000_000, [pltpu.VMEM((16, 128), F32)]
        )(parts, latent.T, projection, attention_out, stats)
    with jax.named_scope("upstream_over_z"):
        gathered = lax.all_to_all(pay, "z", 0, 0)
    with jax.named_scope("main"):
        dq, da, db = call(
            main_kernel,
            [((NZ, 128, 256), BF16), ((NY, 256, 256), BF16), ((NY, 256, 256), BF16)],
            4_000_000_000,
            [pltpu.VMEM((1024, 1024), BF16)],
        )(qg, kva, kvb, gathered, projection)
    with jax.named_scope("dkv_over_core"):
        other = swap(db, "c", NC, 1)
        own, *send = call(
            fold_kernel, [((256, 256), F32)] + [((256, 256), BF16)] * 3, FOLD_COST
        )(da, other)
    with jax.named_scope("dkv_over_y"):
        back = [swap(s, "y", NY, k) for k, s in zip((1, 2, 3), send)]
    with jax.named_scope("dq_over_z"):
        dqs = lax.all_to_all(dq, "z", 0, 0)
    with jax.named_scope("final"):
        return tuple(
            call(final_kernel, [((128, 256), BF16)] * 3, 1_000_000)(own, *back, dqs)
        )


def solution(mesh):
    n_h = min(2, mesh.shape["tp"])
    n_x = mesh.shape["tp"] // n_h
    fine = Mesh(mesh.devices.reshape(NY, NZ, NC, n_x, n_h), ("y", "z", "c", "x", "h"))
    ctx = ("y", "z", "c")
    tp = ("x", "h")
    placed = (
        P(ctx, None),
        P(ctx),
        P(ctx, tp),
        P(ctx, tp),
        P(ctx, tp),
        P(ctx, tp),
        P(tp, None),
    )
    return jax.shard_map(
        functools.partial(local, n_x * n_h),
        mesh=fine,
        in_specs=placed,
        out_specs=(P(ctx, tp), P(ctx, tp), P(ctx, tp)),
        check_vma=False,
    )
```

```python
import functools

import jax
import jax.numpy as jnp
from jax import lax
from jax.experimental import pallas as pl
from jax.experimental.pallas import tpu as pltpu
from jax.sharding import Mesh, PartitionSpec as P

HEAD = 128
SPAN = 64
NZ, NY, NC = 8, 4, 2
NQ = NY * NC
LOG2E = 1.4426950408889634
FACTOR = HEAD ** (-0.5)
SCALE = FACTOR * LOG2E
MASKED = -(2.0**100)
F32 = jnp.float32
BF16 = jnp.bfloat16
NT = (((1,), (1,)), ((), ()))
MIB = 1 << 20
JOIN_COST = 1_000_000
FOLD_COST = 1_000_000


def dot_nt(a, b):
    return lax.dot_general(a, b, NT, preferred_element_type=F32)


def dot(a, b):
    return jnp.dot(a, b, preferred_element_type=F32)


def prep_kernel(
    pos_ref, q_hbm, k_hbm, v_hbm, o_hbm, proj_hbm, qpay_ref, kvpay_ref, part_ref, *scratch
):
    buffers, sems = scratch[:-1], scratch[-1]
    sources = (k_hbm, v_hbm, q_hbm, o_hbm, proj_hbm)
    copies = [
        pltpu.make_async_copy(src, dst, sems.at[n])
        for n, (src, dst) in enumerate(zip(sources, buffers))
    ]
    for copy in copies:
        copy.start()
    k_ref, v_ref, q_ref, o_ref, proj_ref = buffers
    block = lax.shift_right_logical(pos_ref[0], 6).astype(F32)
    tag = jnp.full((16, 256), block, F32).astype(BF16)
    for copy in copies:
        copy.wait()
    k, v = k_ref[...], v_ref[...]
    for i in range(NZ):
        kvpay_ref[i, 0:128, :] = k
        kvpay_ref[i, 128:256, :] = v
        kvpay_ref[i, 256:272, :] = tag
    qpay_ref[0:128, :] = q_ref[...]
    qpay_ref[128:144, :] = tag
    part_ref[...] = dot(o_ref[...], proj_ref[...])


def query_positions(qg_ref):
    lane = lax.broadcasted_iota(jnp.int32, (1, 128), 1)
    low = lane < SPAN
    row = (lane & (SPAN - 1)).astype(F32)
    early, late = [], []
    for p in range(NQ // 2):
        first = qg_ref[2 * p, 128:144, 0:128].astype(F32)[0:1, :]
        second = qg_ref[2 * p + 1, 128:144, 0:128].astype(F32)[0:1, :]
        block = jnp.where(low, first, second)
        early.append(block * SPAN + row)
        late.append((127.0 - block) * SPAN + row)
    return jnp.concatenate(early, axis=1), jnp.concatenate(late, axis=1)


def key_positions(kv_ref, late):
    row = lax.broadcasted_iota(jnp.int32, (SPAN, 128), 0).astype(F32)
    out = []
    for j in range(kv_ref.shape[0]):
        block = kv_ref[j, 256:272, 0:128].astype(F32)[0:1, :]
        base = (127.0 - block) * SPAN if late else block * SPAN
        out.append(base + row)
    column = jnp.concatenate(out, axis=0)
    return jnp.concatenate([column] * 4, axis=1)


def rows_of(ref, start, head):
    part = ref[:, start : start + SPAN, head * HEAD : (head + 1) * HEAD]
    return part.reshape(part.shape[0] * SPAN, HEAD)


def stats_kernel(
    q0_ref, q1_ref, q2_ref, q3_ref, kv_ref, p0_ref, p1_ref, lat_ref, proj_ref, o_ref,
    out_ref, qg_ref, s_ref, st_ref, d_ref,
):
    here = lax.axis_index("y")
    for k, ref in enumerate((q0_ref, q1_ref, q2_ref, q3_ref)):
        for core in range(NC):
            qg_ref[2 * (here ^ k) + core] = ref[core]
    q_early, q_late = query_positions(qg_ref)
    sides = (kv_ref.at[0:4], kv_ref.at[4:8])
    for head in range(2):
        for part in range(2):
            q = rows_of(qg_ref, part * SPAN, head)
            top = None
            units = []
            for n, kv in enumerate(sides):
                units.append((n, kv, 0, part == 0))
                if part == 1:
                    units.append((n + 2, kv, SPAN, True))
            for slot, kv, start, masked in units:
                s = dot_nt(rows_of(kv, start, head), q) * SCALE
                if masked:
                    qp = q_late if start else q_early
                    s = jnp.where(key_positions(kv, start > 0) <= qp, s, MASKED)
                s_ref[slot] = s
                here = jnp.max(s.reshape(32, 8, 512), axis=0)
                top = here if top is None else jnp.maximum(top, here)
            top = jnp.max(top, axis=0, keepdims=True).astype(BF16).astype(F32)
            total = jnp.zeros((8, 512), F32)
            for slot, kv, start, masked in units:
                p = jnp.exp2(s_ref[slot] - top)
                total = total + jnp.sum(p.reshape(32, 8, 512), axis=0)
            total = jnp.sum(total, axis=0, keepdims=True)
            high = total.astype(BF16).astype(F32)
            low = total - high
            base = (head * 2 + part) * 12
            for r in range(4):
                lanes = slice(r * 128, (r + 1) * 128)
                st_ref[base + r : base + r + 1, :] = top[:, lanes]
                st_ref[base + 4 + r : base + 5 + r, :] = high[:, lanes]
                st_ref[base + 8 + r : base + 9 + r, :] = low[:, lanes]
    stats = st_ref[...].astype(BF16)
    coupled = p0_ref[...] + p1_ref[...]
    shifts = coupled[:, 0:64]
    log_scale = coupled[:, 64:128]
    damping = jnp.exp(-log_scale)
    normed = (lat_ref[...].T - shifts) * damping
    upstream = jnp.concatenate([-normed * damping, 1.0 - normed * normed], axis=1).astype(BF16)
    d_ref[...] = jnp.zeros((16, 128), F32)
    for head in range(2):
        cols = slice(head * HEAD, (head + 1) * HEAD)
        grad = dot_nt(upstream, proj_ref[cols, :]).astype(BF16)
        product = grad.astype(F32) * o_ref[:, cols].astype(F32)
        delta = jnp.sum(product.T, axis=0, keepdims=True)
        high = delta.astype(BF16).astype(F32)
        d_ref[2 * head : 2 * head + 1, :] = high
        d_ref[2 * head + 1 : 2 * head + 2, :] = delta - high
    deltas = d_ref[...].astype(BF16)
    for i in range(NQ):
        out_ref[i, 0:128, :] = upstream
        out_ref[i, 128:144, :] = deltas
        out_ref[i, 144:192, :] = stats


def join_kernel(own_ref, recv_ref, out_ref):
    core = lax.axis_index("c")
    out_ref[core] = own_ref[...]
    out_ref[1 - core] = recv_ref[...]


def main_kernel(qg_ref, kv_ref, g_ref, proj_ref, dkv_ref, qa_ref, qb_ref, ds_ref, dq_ref):
    q_early, q_late = query_positions(qg_ref)
    lane = lax.broadcasted_iota(jnp.int32, (1, 128), 1)
    low = lane < SPAN
    upstream = [
        g_ref[:, part * SPAN : (part + 1) * SPAN, :].reshape(NQ * SPAN, HEAD) for part in range(2)
    ]
    tails = [g_ref[i, 128:144, :].astype(F32) for i in range(NQ)]
    turned = [pltpu.roll(t, SPAN, 1) for t in tails]
    stats = g_ref[:, 144:192, :].astype(F32)
    sides = (kv_ref.at[0:4], kv_ref.at[4:8])
    grads = (dkv_ref.at[0:4], dkv_ref.at[4:8])
    for head in range(2):
        cols = slice(head * HEAD, (head + 1) * HEAD)
        proj = proj_ref[cols, :]
        lse, delta, q, dout = [], [], [], []
        for part in range(2):
            base = (head * 2 + part) * 12
            tops = stats[:, base : base + 4, :]
            sums = stats[:, base + 4 : base + 8, :] + stats[:, base + 8 : base + 12, :]
            top = jnp.max(tops, axis=0)
            total = jnp.sum(sums * jnp.exp2(tops - top[None]), axis=0)
            value = top + jnp.log(total) * LOG2E
            lse.append(jnp.concatenate([value[r : r + 1, :] for r in range(4)], axis=1))
            pieces = []
            for p in range(NQ // 2):
                left = (tails if part == 0 else turned)[2 * p]
                right = (turned if part == 0 else tails)[2 * p + 1]
                both = jnp.where(low, left, right)
                pieces.append(both[2 * head : 2 * head + 1, :] + both[2 * head + 1 : 2 * head + 2, :])
            delta.append(jnp.concatenate(pieces, axis=1))
            q.append(rows_of(qg_ref, part * SPAN, head))
            dout.append(dot_nt(upstream[part], proj).astype(BF16))

        def unit(keys, values, kp, part):
            t = dot_nt(keys, q[part]) * SCALE - lse[part]
            if kp is not None:
                t = jnp.where(kp <= (q_late if part else q_early), t, MASKED)
            p = jnp.exp2(t)
            ds = p * (dot_nt(values, dout[part]) - delta[part])
            return p.astype(BF16), ds.astype(BF16)

        for n in range(2):
            kv, grad = sides[n], grads[n]
            keys = rows_of(kv, 0, head)
            values = rows_of(kv, 128, head)
            pe, se = unit(keys, values, key_positions(kv, False), 0)
            ds_ref[n * 256 : (n + 1) * 256, 0:512] = se
            dv = dot(pe, dout[0])
            dk = dot(se, q[0])
            pd, sd = unit(keys, values, None, 1)
            ds_ref[n * 256 : (n + 1) * 256, 512:1024] = sd
            dv = dv + dot(pd, dout[1])
            dk = dk + dot(sd, q[1])
            grad[:, 0:64, cols] = (dk * FACTOR).astype(BF16).reshape(NY, SPAN, HEAD)
            grad[:, 128:192, cols] = dv.astype(BF16).reshape(NY, SPAN, HEAD)
            keys = rows_of(kv, 64, head)
            values = rows_of(kv, 192, head)
            pd, sd = unit(keys, values, key_positions(kv, True), 1)
            ds_ref[512 + n * 256 : 512 + (n + 1) * 256, 512:1024] = sd
            dv = dot(pd, dout[1])
            dk = dot(sd, q[1])
            grad[:, 64:128, cols] = (dk * FACTOR).astype(BF16).reshape(NY, SPAN, HEAD)
            grad[:, 192:256, cols] = dv.astype(BF16).reshape(NY, SPAN, HEAD)
        early_t = jnp.concatenate([rows_of(kv, 0, head) for kv in sides], axis=0).T
        late_t = jnp.concatenate([rows_of(kv, 64, head) for kv in sides], axis=0).T
        dqe = dot(early_t, ds_ref[0:512, 0:512])
        dql = dot(early_t, ds_ref[0:512, 512:1024]) + dot(late_t, ds_ref[512:1024, 512:1024])
        dq_ref[:, 0:64, cols] = (dqe * FACTOR).T.astype(BF16).reshape(NQ, SPAN, HEAD)
        dq_ref[:, 64:128, cols] = (dql * FACTOR).T.astype(BF16).reshape(NQ, SPAN, HEAD)
    core = lax.axis_index("c")
    for y in range(NY):
        qa_ref[y] = dq_ref[2 * y + core]
        qb_ref[y] = dq_ref[2 * y + 1 - core]


def fold_kernel(own_ref, recv_ref, o0_ref, o1_ref, o2_ref, o3_ref):
    here = lax.axis_index("y")
    for k, ref in enumerate((o0_ref, o1_ref, o2_ref, o3_ref)):
        total = own_ref[here ^ k].astype(F32) + recv_ref[here ^ k].astype(F32)
        ref[...] = total.astype(ref.dtype)


def final_kernel(own_ref, r1_ref, r2_ref, r3_ref, kv_ref, qo_ref, ko_ref, vo_ref):
    total = own_ref[...]
    for ref in (r1_ref, r2_ref, r3_ref):
        total = total + ref[...].astype(F32)
    qo_ref[...] = total.astype(BF16)
    total = kv_ref[0].astype(F32)
    for i in range(1, NZ):
        total = total + kv_ref[i].astype(F32)
    ko_ref[...] = total[0:128, :].astype(BF16)
    vo_ref[...] = total[128:256, :].astype(BF16)


def call(kernel, outs, cost, scratch=(), specs=None, limit=48):
    vmem = pl.BlockSpec(memory_space=pltpu.VMEM)

    def run(*args):
        return pl.pallas_call(
            kernel,
            out_shape=[jax.ShapeDtypeStruct(s, d) for s, d in outs],
            in_specs=specs or [vmem] * len(args),
            out_specs=[vmem] * len(outs),
            scratch_shapes=list(scratch),
            compiler_params=pltpu.CompilerParams(vmem_limit_bytes=limit * MIB),
            cost_estimate=pl.CostEstimate(flops=cost, bytes_accessed=2 * MIB, transcendentals=0),
        )(*args)

    return run


def swap(x, axis, size, k):
    return lax.ppermute(x, axis, [(i, i ^ k) for i in range(size)])


def local(n_tp, latent, positions, queries, keys, values, attention_out, projection):
    hbm = pl.BlockSpec(memory_space=pltpu.HBM)
    with jax.named_scope("prep"):
        qpay, kvpay, total = call(
            prep_kernel,
            [((144, 256), BF16), ((NZ, 272, 256), BF16), ((128, 128), F32)],
            10_000_000,
            [pltpu.VMEM((128, 256), BF16)] * 4
            + [pltpu.VMEM((256, 128), BF16), pltpu.SemaphoreType.DMA((5,))],
            [pl.BlockSpec(memory_space=pltpu.SMEM)] + [hbm] * 5,
            limit=62,
        )(positions, queries, keys, values, attention_out, projection)
    with jax.named_scope("kv_over_z"):
        kvg = lax.all_to_all(kvpay, "z", 0, 0)
    with jax.named_scope("coupled_over_h"):
        near = [swap(total, ("x", "h"), n_tp, k) for k in (1, 2, 3) if k < n_tp]
        total = sum(near, total)
    with jax.named_scope("q_over_core"):
        other = swap(qpay, "c", NC, 1)
        (pair,) = call(join_kernel, [((NC, 144, 256), BF16)], JOIN_COST)(qpay, other)
    with jax.named_scope("q_over_y"):
        arrived = [swap(pair, "y", NY, k) for k in (1, 2, 3)]
    with jax.named_scope("coupled_over_x"):
        far = swap(total, ("x", "h"), n_tp, 4) if n_tp > 4 else jnp.zeros_like(total)
    with jax.named_scope("stats"):
        pay, qg = call(
            stats_kernel,
            [((NQ, 192, 128), BF16), ((NQ, 144, 256), BF16)],
            1_000_000_000,
            [
                pltpu.VMEM((4, 256, 512), F32),
                pltpu.VMEM((48, 128), F32),
                pltpu.VMEM((16, 128), F32),
            ],
        )(pair, *arrived, kvg, total, far, latent.T, projection, attention_out)
    with jax.named_scope("upstream_over_yc"):
        gathered = lax.all_to_all(pay, ("y", "c"), 0, 0)
    with jax.named_scope("main"):
        dkv, dqa, dqb = call(
            main_kernel,
            [((NZ, 256, 256), BF16), ((NY, 128, 256), BF16), ((NY, 128, 256), BF16)],
            4_000_000_000,
            [pltpu.VMEM((1024, 1024), BF16), pltpu.VMEM((NQ, 128, 256), BF16)],
        )(qg, kvg, gathered, projection)
    with jax.named_scope("dkv_over_z"):
        dkvs = lax.all_to_all(dkv, "z", 0, 0)
    with jax.named_scope("dq_over_core"):
        other = swap(dqb, "c", NC, 1)
        own, *send = call(
            fold_kernel, [((128, 256), F32)] + [((128, 256), BF16)] * 3, FOLD_COST
        )(dqa, other)
    with jax.named_scope("dq_over_y"):
        back = [swap(s, "y", NY, k) for k, s in zip((1, 2, 3), send)]
    with jax.named_scope("final"):
        return tuple(
            call(final_kernel, [((128, 256), BF16)] * 3, 1_000_000)(own, *back, dkvs)
        )


def solution(mesh):
    n_h = min(2, mesh.shape["tp"])
    n_x = mesh.shape["tp"] // n_h
    fine = Mesh(mesh.devices.reshape(NY, NZ, NC, n_x, n_h), ("y", "z", "c", "x", "h"))
    ctx = ("y", "z", "c")
    tp = ("x", "h")
    placed = (
        P(ctx, None),
        P(ctx),
        P(ctx, tp),
        P(ctx, tp),
        P(ctx, tp),
        P(ctx, tp),
        P(tp, None),
    )
    return jax.shard_map(
        functools.partial(local, n_x * n_h),
        mesh=fine,
        in_specs=placed,
        out_specs=(P(ctx, tp), P(ctx, tp), P(ctx, tp)),
        check_vma=False,
    )
```

```python
import functools

import jax
import jax.numpy as jnp
from jax import lax
from jax.experimental import pallas as pl
from jax.experimental.pallas import tpu as pltpu
from jax.sharding import Mesh, PartitionSpec as P

HEAD = 128
SPAN = 64
NZ, NY, NC = 8, 4, 2
LOG2E = 1.4426950408889634
FACTOR = HEAD ** (-0.5)
SCALE = FACTOR * LOG2E
MASKED = -(2.0**100)
F32 = jnp.float32
BF16 = jnp.bfloat16
NT = (((1,), (1,)), ((), ()))
MIB = 1 << 20
JOIN_COST = 1_000_000
PAIR_COST = 2_000_000_000
FOLD_COST = 20_000_000_000


def dot_nt(a, b):
    return lax.dot_general(a, b, NT, preferred_element_type=F32)


def dot(a, b):
    return jnp.dot(a, b, preferred_element_type=F32)


def prep_kernel(
    pos_ref, q_hbm, k_hbm, v_hbm, o_hbm, proj_hbm, qpay_ref, kvpay_ref, part_ref, *scratch
):
    buffers, sems = scratch[:-1], scratch[-1]
    sources = (k_hbm, v_hbm, q_hbm, o_hbm, proj_hbm)
    copies = [
        pltpu.make_async_copy(src, dst, sems.at[n])
        for n, (src, dst) in enumerate(zip(sources, buffers))
    ]
    for copy in copies:
        copy.start()
    k_ref, v_ref, q_ref, o_ref, proj_ref = buffers
    block = lax.shift_right_logical(pos_ref[0], 6).astype(F32)
    tag = jnp.full((16, 256), block, F32).astype(BF16)
    for copy in copies:
        copy.wait()
    k, v, q = k_ref[...], v_ref[...], q_ref[...]
    kvpay_ref[0:128, :] = k
    kvpay_ref[128:256, :] = v
    kvpay_ref[256:272, :] = tag
    for i in range(NZ):
        qpay_ref[i, 0:128, :] = q
        qpay_ref[i, 128:144, :] = tag
    part_ref[...] = dot(o_ref[...], proj_ref[...])


def query_positions(qg_ref):
    lane = lax.broadcasted_iota(jnp.int32, (1, 128), 1)
    low = lane < SPAN
    row = (lane & (SPAN - 1)).astype(F32)
    early, late = [], []
    for p in range(NZ // 2):
        first = qg_ref[2 * p, 128:144, 0:128].astype(F32)[0:1, :]
        second = qg_ref[2 * p + 1, 128:144, 0:128].astype(F32)[0:1, :]
        block = jnp.where(low, first, second)
        early.append(block * SPAN + row)
        late.append((127.0 - block) * SPAN + row)
    return jnp.concatenate(early, axis=1), jnp.concatenate(late, axis=1)


def key_positions(kv_ref, late):
    row = lax.broadcasted_iota(jnp.int32, (SPAN, 128), 0).astype(F32)
    out = []
    for j in range(NY):
        block = kv_ref[j, 256:272, 0:128].astype(F32)[0:1, :]
        base = (127.0 - block) * SPAN if late else block * SPAN
        out.append(base + row)
    column = jnp.concatenate(out, axis=0)
    return jnp.concatenate([column] * 4, axis=1)


def rows_of(ref, start, head):
    part = ref[:, start : start + SPAN, head * HEAD : (head + 1) * HEAD]
    return part.reshape(part.shape[0] * SPAN, HEAD)


def stats_kernel(
    qg_ref, kva_ref, kvb_ref, p0_ref, p1_ref, p2_ref, p3_ref, lat_ref, proj_ref, o_ref,
    out_ref, prob_ref, top_ref, s_ref, tail_ref,
):
    tail_ref[...] = jnp.zeros((48, 128), F32)
    q_early, q_late = query_positions(qg_ref)
    sides = (kva_ref, kvb_ref)
    for head in range(2):
        for part in range(2):
            q = rows_of(qg_ref, part * SPAN, head)
            top = None
            units = []
            for n, kv in enumerate(sides):
                units.append((n, kv, 0, part == 0))
                if part == 1:
                    units.append((n + 2, kv, SPAN, True))
            for slot, kv, start, masked in units:
                s = dot_nt(rows_of(kv, start, head), q) * SCALE
                if masked:
                    qp = q_late if start else q_early
                    s = jnp.where(key_positions(kv, start > 0) <= qp, s, MASKED)
                s_ref[slot] = s
                here = jnp.max(s.reshape(32, 8, 512), axis=0)
                top = here if top is None else jnp.maximum(top, here)
            top = jnp.max(top, axis=0, keepdims=True)
            total = jnp.zeros((8, 512), F32)
            for slot, kv, start, masked in units:
                p = jnp.exp2(s_ref[slot] - top)
                total = total + jnp.sum(p.reshape(32, 8, 512), axis=0)
                rows = slice(slot * 256, (slot + 1) * 256)
                prob_ref[head, rows, part * 512 : (part + 1) * 512] = p.astype(BF16)
            total = jnp.sum(total, axis=0, keepdims=True)
            lse = top + jnp.log(total) * LOG2E
            high = lse.astype(BF16).astype(F32)
            low = lse - high
            group = head * 2 + part
            for r in range(4):
                lanes = slice(r * 128, (r + 1) * 128)
                top_ref[group * 4 + r : group * 4 + r + 1, :] = top[:, lanes]
                row = 8 + group * 8 + r
                tail_ref[row : row + 1, :] = high[:, lanes]
                tail_ref[row + 4 : row + 5, :] = low[:, lanes]
    coupled = (p0_ref[...] + p1_ref[...]) + (p2_ref[...] + p3_ref[...])
    shifts = coupled[:, 0:64]
    log_scale = coupled[:, 64:128]
    damping = jnp.exp(-log_scale)
    normed = (lat_ref[...].T - shifts) * damping
    upstream = jnp.concatenate([-normed * damping, 1.0 - normed * normed], axis=1).astype(BF16)
    for head in range(2):
        cols = slice(head * HEAD, (head + 1) * HEAD)
        grad = dot_nt(upstream, proj_ref[cols, :]).astype(BF16)
        product = grad.astype(F32) * o_ref[:, cols].astype(F32)
        delta = jnp.sum(product.T, axis=0, keepdims=True)
        high = delta.astype(BF16).astype(F32)
        tail_ref[2 * head : 2 * head + 1, :] = high
        tail_ref[2 * head + 1 : 2 * head + 2, :] = delta - high
    tail = tail_ref[...].astype(BF16)
    for i in range(NZ):
        out_ref[i, 0:128, :] = upstream
        out_ref[i, 128:176, :] = tail


def pair_kernel(own_ref, far_ref, after_ref, out_ref):
    out_ref[0] = own_ref[...]
    out_ref[1] = far_ref[...]


def join_kernel(own_ref, recv_ref, *refs):
    kv_ref = refs[-1]
    for n in range(2):
        kv_ref[2 * n] = own_ref[n]
        kv_ref[2 * n + 1] = recv_ref[n]


def main_kernel(
    qg_ref, kva_ref, kvb_ref, g_ref, proj_ref, prob_ref, top_ref, dq_ref, da_ref, db_ref, ds_ref
):
    low = lax.broadcasted_iota(jnp.int32, (1, 128), 1) < SPAN
    upstream = [
        g_ref[:, part * SPAN : (part + 1) * SPAN, :].reshape(NZ * SPAN, HEAD) for part in range(2)
    ]
    tails = g_ref[:, 128:176, :].astype(F32)
    deltas = [tails[i, 0:8, :] for i in range(NZ)]
    turned = [pltpu.roll(t, SPAN, 1) for t in deltas]
    sides = (kva_ref, kvb_ref)
    grads = (da_ref, db_ref)
    for head in range(2):
        cols = slice(head * HEAD, (head + 1) * HEAD)
        proj = proj_ref[cols, :]
        delta, q, dout = [], [], []
        for part in range(2):
            group = head * 2 + part
            row = 8 + group * 8
            partial = tails[:, row : row + 4, :] + tails[:, row + 4 : row + 8, :]
            top = jnp.max(partial, axis=0)
            total = jnp.sum(jnp.exp2(partial - top[None]), axis=0)
            lse = top + jnp.log(total) * LOG2E
            weight = jnp.exp2(top_ref[group * 4 : group * 4 + 4, :] - lse)
            lanes, column = [], []
            for p in range(NZ // 2):
                left = (deltas if part == 0 else turned)[2 * p]
                right = (turned if part == 0 else deltas)[2 * p + 1]
                both = jnp.where(low, left, right)
                here = both[2 * head : 2 * head + 1, :] + both[2 * head + 1 : 2 * head + 2, :]
                lanes.append(here * weight[p : p + 1, :])
                column.append(jnp.broadcast_to(weight[p : p + 1, :], (128, 128)).T)
            delta.append(jnp.concatenate(lanes, axis=1))
            q.append(rows_of(qg_ref, part * SPAN, head))
            grad = dot_nt(upstream[part], proj).astype(BF16).astype(F32)
            dout.append((grad * jnp.concatenate(column, axis=0)).astype(BF16))
        q_all = jnp.concatenate(q, axis=0)
        dout_all = jnp.concatenate(dout, axis=0)

        def unit(rows, part, values):
            span = slice(part * 512, (part + 1) * 512)
            p = prob_ref[head, rows, span].astype(F32)
            ds_ref[rows, span] = (p * (dot_nt(values, dout[part]) - delta[part])).astype(BF16)

        for n in range(2):
            kv, grad = sides[n], grads[n]
            rows = slice(n * 256, (n + 1) * 256)
            values = rows_of(kv, 128, head)
            unit(rows, 0, values)
            unit(rows, 1, values)
            dv = dot(prob_ref[head, rows, :], dout_all)
            dk = dot(ds_ref[rows, :], q_all)
            grad[:, 0:64, cols] = (dk * FACTOR).astype(BF16).reshape(NY, SPAN, HEAD)
            grad[:, 128:192, cols] = dv.astype(BF16).reshape(NY, SPAN, HEAD)
            rows = slice(512 + n * 256, 512 + (n + 1) * 256)
            unit(rows, 1, rows_of(kv, 192, head))
            dv = dot(prob_ref[head, rows, 512:1024], dout[1])
            dk = dot(ds_ref[rows, 512:1024], q[1])
            grad[:, 64:128, cols] = (dk * FACTOR).astype(BF16).reshape(NY, SPAN, HEAD)
            grad[:, 192:256, cols] = dv.astype(BF16).reshape(NY, SPAN, HEAD)
        early_t = jnp.concatenate([rows_of(kv, 0, head) for kv in sides], axis=0).T
        late_t = jnp.concatenate([rows_of(kv, 64, head) for kv in sides], axis=0).T
        dqe = dot(early_t, ds_ref[0:512, 0:512])
        dql = dot(early_t, ds_ref[0:512, 512:1024]) + dot(late_t, ds_ref[512:1024, 512:1024])
        dq_ref[:, 0:64, cols] = (dqe * FACTOR).T.astype(BF16).reshape(NZ, SPAN, HEAD)
        dq_ref[:, 64:128, cols] = (dql * FACTOR).T.astype(BF16).reshape(NZ, SPAN, HEAD)


def fold_kernel(own_ref, recv_ref, o0_ref, o1_ref, o2_ref, o3_ref):
    o0_ref[...] = own_ref[0].astype(F32) + recv_ref[0].astype(F32)
    for k, ref in ((1, o1_ref), (2, o2_ref), (3, o3_ref)):
        ref[...] = (own_ref[k].astype(F32) + recv_ref[k].astype(F32)).astype(BF16)


def final_kernel(own_ref, r1_ref, r2_ref, r3_ref, dq_ref, qo_ref, ko_ref, vo_ref):
    total = own_ref[...]
    for ref in (r1_ref, r2_ref, r3_ref):
        total = total + ref[...].astype(F32)
    ko_ref[...] = total[0:128, :].astype(BF16)
    vo_ref[...] = total[128:256, :].astype(BF16)
    dq = dq_ref[0].astype(F32)
    for i in range(1, NZ):
        dq = dq + dq_ref[i].astype(F32)
    qo_ref[...] = dq.astype(BF16)


def call(kernel, outs, cost, scratch=(), specs=None, limit=48):
    vmem = pl.BlockSpec(memory_space=pltpu.VMEM)

    def run(*args):
        return pl.pallas_call(
            kernel,
            out_shape=[jax.ShapeDtypeStruct(s, d) for s, d in outs],
            in_specs=specs or [vmem] * len(args),
            out_specs=[vmem] * len(outs),
            scratch_shapes=list(scratch),
            compiler_params=pltpu.CompilerParams(vmem_limit_bytes=limit * MIB),
            cost_estimate=pl.CostEstimate(flops=cost, bytes_accessed=2 * MIB, transcendentals=0),
        )(*args)

    return run


def swap(x, axis, size, k):
    return lax.ppermute(x, axis, [(i, i ^ k) for i in range(size)])


def local(n_x, n_h, latent, positions, queries, keys, values, attention_out, projection):
    with jax.named_scope("prep"):
        qpay, kvpay, total = call(
            prep_kernel,
            [((NZ, 144, 256), BF16), ((272, 256), BF16), ((128, 128), F32)],
            10_000_000,
            [pltpu.VMEM((128, 256), BF16)] * 4
            + [pltpu.VMEM((256, 128), BF16), pltpu.SemaphoreType.DMA((5,))],
            [pl.BlockSpec(memory_space=pltpu.SMEM)] + [pl.BlockSpec(memory_space=pltpu.HBM)] * 5,
            limit=62,
        )(positions, queries, keys, values, attention_out, projection)
    with jax.named_scope("q_over_z"):
        qg = lax.all_to_all(qpay, "z", 0, 0)
    with jax.named_scope("coupled_over_h"):
        total = total + swap(total, "h", n_h, 1) if n_h > 1 else total
    with jax.named_scope("coupled_over_x"):
        if n_x > 1:
            parts = [swap(total, "x", n_x, k) for k in (1, 2, 3)]
        else:
            parts = [jnp.zeros_like(total)] * 3
    with jax.named_scope("kv_over_y"):
        (pair,) = call(pair_kernel, [((2, 272, 256), BF16)], PAIR_COST)(
            kvpay, swap(kvpay, "y", NY, 2), total
        )
        other = swap(pair, "y", NY, 1)
    with jax.named_scope("join"):
        (kva,) = call(join_kernel, [((NY, 272, 256), BF16)], JOIN_COST)(pair, other, *parts)
    with jax.named_scope("kv_over_core"):
        kvb = swap(kva, "c", NC, 1)
    with jax.named_scope("stats"):
        pay, prob, top = call(
            stats_kernel,
            [((NZ, 176, 128), BF16), ((2, 1024, 1024), BF16), ((16, 128), F32)],
            1_000_000_000,
            [pltpu.VMEM((4, 256, 512), F32), pltpu.VMEM((48, 128), F32)],
            limit=24,
        )(qg, kva, kvb, total, *parts, latent.T, projection, attention_out)
    with jax.named_scope("upstream_over_z"):
        gathered = lax.all_to_all(pay, "z", 0, 0)
    with jax.named_scope("main"):
        dq, da, db = call(
            main_kernel,
            [((NZ, 128, 256), BF16), ((NY, 256, 256), BF16), ((NY, 256, 256), BF16)],
            4_000_000_000,
            [pltpu.VMEM((1024, 1024), BF16)],
            limit=24,
        )(qg, kva, kvb, gathered, projection, prob, top)
    with jax.named_scope("dkv_over_core"):
        other = swap(db, "c", NC, 1)
        own, *send = call(
            fold_kernel, [((256, 256), F32)] + [((256, 256), BF16)] * 3, FOLD_COST
        )(da, other)
    with jax.named_scope("dkv_over_y"):
        back = [swap(s, "y", NY, k) for k, s in zip((3, 2, 1), (send[2], send[1], send[0]))]
    with jax.named_scope("dq_over_z"):
        dqs = lax.all_to_all(dq, "z", 0, 0)
    with jax.named_scope("final"):
        return tuple(
            call(final_kernel, [((128, 256), BF16)] * 3, 1_000_000)(own, *back, dqs)
        )


def solution(mesh):
    n_h = min(2, mesh.shape["tp"])
    n_x = mesh.shape["tp"] // n_h
    fine = Mesh(mesh.devices.reshape(NY, NZ, NC, n_x, n_h), ("y", "z", "c", "x", "h"))
    ctx = ("y", "z", "c")
    tp = ("x", "h")
    placed = (
        P(ctx, None),
        P(ctx),
        P(ctx, tp),
        P(ctx, tp),
        P(ctx, tp),
        P(ctx, tp),
        P(tp, None),
    )
    return jax.shard_map(
        functools.partial(local, n_x, n_h),
        mesh=fine,
        in_specs=placed,
        out_specs=(P(ctx, tp), P(ctx, tp), P(ctx, tp)),
        check_vma=False,
    )
```

```python
import functools

import jax
import jax.numpy as jnp
from jax import lax
from jax.experimental import pallas as pl
from jax.experimental.pallas import tpu as pltpu
from jax.sharding import Mesh, PartitionSpec as P

HEAD = 128
SPAN = 64
NZ, NY, NC = 8, 4, 2
LOG2E = 1.4426950408889634
FACTOR = HEAD ** (-0.5)
SCALE = FACTOR * LOG2E
MASKED = -(2.0**100)
F32 = jnp.float32
BF16 = jnp.bfloat16
NT = (((1,), (1,)), ((), ()))
MIB = 1 << 20
RING_Q = [[0, 1, 2, 3, 4, 5, 6, 7]]
RING_P = [[7, 6, 5, 4, 3, 2, 1, 0]]
RING_D = [[0, 1, 2, 3, 4, 5, 6, 7]]
ORDER = (7, 6, 5, 4, 3, 2, 1, 0)
BACK = (0, 1, 2, 3, 4, 5, 6, 7)
JOIN_COST = 1_000_000
PAIR_COST = 5_000_000_000
ADD_COST = 1_000_000_000
FOLD_COST = 20_000_000_000


def dot_nt(a, b):
    return lax.dot_general(a, b, NT, preferred_element_type=F32)


def dot(a, b):
    return jnp.dot(a, b, preferred_element_type=F32)


def prep_kernel(
    pos_ref, q_hbm, k_hbm, v_hbm, o_hbm, proj_hbm, qpay_ref, kvpay_ref, part_ref, *scratch
):
    buffers, sems = scratch[:-1], scratch[-1]
    sources = (k_hbm, v_hbm, q_hbm, o_hbm, proj_hbm)
    copies = [
        pltpu.make_async_copy(src, dst, sems.at[n])
        for n, (src, dst) in enumerate(zip(sources, buffers))
    ]
    for copy in copies:
        copy.start()
    k_ref, v_ref, q_ref, o_ref, proj_ref = buffers
    block = lax.shift_right_logical(pos_ref[0], 6).astype(F32)
    tag = jnp.full((16, 256), block, F32).astype(BF16)
    for copy in copies:
        copy.wait()
    k, v, q = k_ref[...], v_ref[...], q_ref[...]
    kvpay_ref[0:128, :] = k
    kvpay_ref[128:256, :] = v
    kvpay_ref[256:272, :] = tag
    for i in range(NZ):
        qpay_ref[i, 0:128, :] = q
        qpay_ref[i, 128:144, :] = tag
    part_ref[...] = dot(o_ref[...], proj_ref[...])


def query_positions(qg_ref):
    lane = lax.broadcasted_iota(jnp.int32, (1, 128), 1)
    low = lane < SPAN
    row = (lane & (SPAN - 1)).astype(F32)
    early, late = [], []
    for p in range(NZ // 2):
        first = qg_ref[2 * p, 128:144, 0:128].astype(F32)[0:1, :]
        second = qg_ref[2 * p + 1, 128:144, 0:128].astype(F32)[0:1, :]
        block = jnp.where(low, first, second)
        early.append(block * SPAN + row)
        late.append((127.0 - block) * SPAN + row)
    return jnp.concatenate(early, axis=1), jnp.concatenate(late, axis=1)


def key_positions(kv_ref, late):
    row = lax.broadcasted_iota(jnp.int32, (SPAN, 128), 0).astype(F32)
    out = []
    for j in range(NY):
        block = kv_ref[j, 256:272, 0:128].astype(F32)[0:1, :]
        base = (127.0 - block) * SPAN if late else block * SPAN
        out.append(base + row)
    column = jnp.concatenate(out, axis=0)
    return jnp.concatenate([column] * 4, axis=1)


def rows_of(ref, start, head):
    part = ref[:, start : start + SPAN, head * HEAD : (head + 1) * HEAD]
    return part.reshape(part.shape[0] * SPAN, HEAD)


def stats_kernel(
    qg_ref, kva_ref, kvb_ref, p0_ref, p1_ref, p2_ref, p3_ref, lat_ref, proj_ref, o_ref,
    out_ref, prob_ref, top_ref, s_ref, tail_ref,
):
    tail_ref[...] = jnp.zeros((48, 128), F32)
    q_early, q_late = query_positions(qg_ref)
    sides = (kva_ref, kvb_ref)
    for head in range(2):
        for part in range(2):
            q = rows_of(qg_ref, part * SPAN, head)
            top = None
            units = []
            for n, kv in enumerate(sides):
                units.append((n, kv, 0, part == 0))
                if part == 1:
                    units.append((n + 2, kv, SPAN, True))
            for slot, kv, start, masked in units:
                s = dot_nt(rows_of(kv, start, head), q) * SCALE
                if masked:
                    qp = q_late if start else q_early
                    s = jnp.where(key_positions(kv, start > 0) <= qp, s, MASKED)
                s_ref[slot] = s
                here = jnp.max(s.reshape(32, 8, 512), axis=0)
                top = here if top is None else jnp.maximum(top, here)
            top = jnp.max(top, axis=0, keepdims=True)
            total = jnp.zeros((8, 512), F32)
            for slot, kv, start, masked in units:
                p = jnp.exp2(s_ref[slot] - top)
                total = total + jnp.sum(p.reshape(32, 8, 512), axis=0)
                rows = slice(slot * 256, (slot + 1) * 256)
                prob_ref[head, rows, part * 512 : (part + 1) * 512] = p.astype(BF16)
            total = jnp.sum(total, axis=0, keepdims=True)
            lse = top + jnp.log(total) * LOG2E
            high = lse.astype(BF16).astype(F32)
            low = lse - high
            group = head * 2 + part
            for r in range(4):
                lanes = slice(r * 128, (r + 1) * 128)
                top_ref[group * 4 + r : group * 4 + r + 1, :] = top[:, lanes]
                row = 8 + group * 8 + r
                tail_ref[row : row + 1, :] = high[:, lanes]
                tail_ref[row + 4 : row + 5, :] = low[:, lanes]
    coupled = (p0_ref[...] + p1_ref[...]) + (p2_ref[...] + p3_ref[...])
    shifts = coupled[:, 0:64]
    log_scale = coupled[:, 64:128]
    damping = jnp.exp(-log_scale)
    normed = (lat_ref[...].T - shifts) * damping
    upstream = jnp.concatenate([-normed * damping, 1.0 - normed * normed], axis=1).astype(BF16)
    for head in range(2):
        cols = slice(head * HEAD, (head + 1) * HEAD)
        grad = dot_nt(upstream, proj_ref[cols, :]).astype(BF16)
        product = grad.astype(F32) * o_ref[:, cols].astype(F32)
        delta = jnp.sum(product.T, axis=0, keepdims=True)
        high = delta.astype(BF16).astype(F32)
        tail_ref[2 * head : 2 * head + 1, :] = high
        tail_ref[2 * head + 1 : 2 * head + 2, :] = delta - high
    tail = tail_ref[...].astype(BF16)
    for i in range(NZ):
        out_ref[i, 0:128, :] = upstream
        out_ref[i, 128:176, :] = tail


def add_kernel(a_ref, b_ref, out_ref):
    out_ref[...] = a_ref[...] + b_ref[...]


def pair_kernel(own_ref, far_ref, after_ref, out_ref):
    del after_ref
    out_ref[0] = own_ref[...]
    out_ref[1] = far_ref[...]


def join_kernel(own_ref, recv_ref, *refs):
    kv_ref = refs[-1]
    for n in range(2):
        kv_ref[2 * n] = own_ref[n]
        kv_ref[2 * n + 1] = recv_ref[n]


def main_kernel(
    qg_ref, kva_ref, kvb_ref, g_ref, proj_ref, prob_ref, top_ref, dq_ref, da_ref, db_ref, ds_ref
):
    low = lax.broadcasted_iota(jnp.int32, (1, 128), 1) < SPAN
    upstream = [
        jnp.concatenate([g_ref[i, part * SPAN : (part + 1) * SPAN, :] for i in ORDER], axis=0)
        for part in range(2)
    ]
    tails = g_ref[:, 128:176, :].astype(F32)
    deltas = [tails[i, 0:8, :] for i in ORDER]
    turned = [pltpu.roll(t, SPAN, 1) for t in deltas]
    sides = (kva_ref, kvb_ref)
    grads = (da_ref, db_ref)
    for head in range(2):
        cols = slice(head * HEAD, (head + 1) * HEAD)
        proj = proj_ref[cols, :]
        delta, q, dout = [], [], []
        for part in range(2):
            group = head * 2 + part
            row = 8 + group * 8
            partial = tails[:, row : row + 4, :] + tails[:, row + 4 : row + 8, :]
            top = jnp.max(partial, axis=0)
            total = jnp.sum(jnp.exp2(partial - top[None]), axis=0)
            lse = top + jnp.log(total) * LOG2E
            weight = jnp.exp2(top_ref[group * 4 : group * 4 + 4, :] - lse)
            lanes, column = [], []
            for p in range(NZ // 2):
                left = (deltas if part == 0 else turned)[2 * p]
                right = (turned if part == 0 else deltas)[2 * p + 1]
                both = jnp.where(low, left, right)
                here = both[2 * head : 2 * head + 1, :] + both[2 * head + 1 : 2 * head + 2, :]
                lanes.append(here * weight[p : p + 1, :])
                column.append(jnp.broadcast_to(weight[p : p + 1, :], (128, 128)).T)
            delta.append(jnp.concatenate(lanes, axis=1))
            q.append(rows_of(qg_ref, part * SPAN, head))
            grad = dot_nt(upstream[part], proj).astype(BF16).astype(F32)
            dout.append((grad * jnp.concatenate(column, axis=0)).astype(BF16))
        q_all = jnp.concatenate(q, axis=0)
        dout_all = jnp.concatenate(dout, axis=0)

        def unit(rows, part, values):
            span = slice(part * 512, (part + 1) * 512)
            p = prob_ref[head, rows, span].astype(F32)
            ds_ref[rows, span] = (p * (dot_nt(values, dout[part]) - delta[part])).astype(BF16)

        for n in range(2):
            kv, grad = sides[n], grads[n]
            rows = slice(n * 256, (n + 1) * 256)
            values = rows_of(kv, 128, head)
            unit(rows, 0, values)
            unit(rows, 1, values)
            dv = dot(prob_ref[head, rows, :], dout_all)
            dk = dot(ds_ref[rows, :], q_all)
            grad[:, 0:64, cols] = (dk * FACTOR).astype(BF16).reshape(NY, SPAN, HEAD)
            grad[:, 128:192, cols] = dv.astype(BF16).reshape(NY, SPAN, HEAD)
            rows = slice(512 + n * 256, 512 + (n + 1) * 256)
            unit(rows, 1, rows_of(kv, 192, head))
            dv = dot(prob_ref[head, rows, 512:1024], dout[1])
            dk = dot(ds_ref[rows, 512:1024], q[1])
            grad[:, 64:128, cols] = (dk * FACTOR).astype(BF16).reshape(NY, SPAN, HEAD)
            grad[:, 192:256, cols] = dv.astype(BF16).reshape(NY, SPAN, HEAD)
        early_t = jnp.concatenate([rows_of(kv, 0, head) for kv in sides], axis=0).T
        late_t = jnp.concatenate([rows_of(kv, 64, head) for kv in sides], axis=0).T
        dqe = dot(early_t, ds_ref[0:512, 0:512])
        dql = dot(early_t, ds_ref[0:512, 512:1024]) + dot(late_t, ds_ref[512:1024, 512:1024])
        dqe = (dqe * FACTOR).T.astype(BF16)
        dql = (dql * FACTOR).T.astype(BF16)
        for i, place in enumerate(BACK):
            dq_ref[place, 0:64, cols] = dqe[i * SPAN : (i + 1) * SPAN, :]
            dq_ref[place, 64:128, cols] = dql[i * SPAN : (i + 1) * SPAN, :]


def fold_kernel(own_ref, recv_ref, o0_ref, o1_ref, o2_ref, o3_ref):
    o0_ref[...] = own_ref[0].astype(F32) + recv_ref[0].astype(F32)
    for k, ref in ((1, o1_ref), (2, o2_ref), (3, o3_ref)):
        ref[...] = (own_ref[k].astype(F32) + recv_ref[k].astype(F32)).astype(BF16)


def final_kernel(own_ref, r1_ref, r2_ref, r3_ref, dq_ref, qo_ref, ko_ref, vo_ref):
    total = own_ref[...]
    for ref in (r1_ref, r2_ref, r3_ref):
        total = total + ref[...].astype(F32)
    ko_ref[...] = total[0:128, :].astype(BF16)
    vo_ref[...] = total[128:256, :].astype(BF16)
    dq = dq_ref[0].astype(F32)
    for i in range(1, NZ):
        dq = dq + dq_ref[i].astype(F32)
    qo_ref[...] = dq.astype(BF16)


def call(kernel, outs, cost, scratch=(), specs=None, limit=48):
    vmem = pl.BlockSpec(memory_space=pltpu.VMEM)

    def run(*args):
        return pl.pallas_call(
            kernel,
            out_shape=[jax.ShapeDtypeStruct(s, d) for s, d in outs],
            in_specs=specs or [vmem] * len(args),
            out_specs=[vmem] * len(outs),
            scratch_shapes=list(scratch),
            compiler_params=pltpu.CompilerParams(vmem_limit_bytes=limit * MIB),
            cost_estimate=pl.CostEstimate(flops=cost, bytes_accessed=2 * MIB, transcendentals=0),
        )(*args)

    return run


def swap(x, axis, size, k):
    return lax.ppermute(x, axis, [(i, i ^ k) for i in range(size)])


def local(n_x, n_h, latent, positions, queries, keys, values, attention_out, projection):
    with jax.named_scope("prep"):
        qpay, kvpay, total = call(
            prep_kernel,
            [((NZ, 144, 256), BF16), ((272, 256), BF16), ((128, 128), F32)],
            10_000_000,
            [pltpu.VMEM((128, 256), BF16)] * 4
            + [pltpu.VMEM((256, 128), BF16), pltpu.SemaphoreType.DMA((5,))],
            [pl.BlockSpec(memory_space=pltpu.SMEM)] + [pl.BlockSpec(memory_space=pltpu.HBM)] * 5,
            limit=62,
        )(positions, queries, keys, values, attention_out, projection)
    with jax.named_scope("q_over_z"):
        qg = lax.all_to_all(qpay, "z", 0, 0, axis_index_groups=RING_Q)
    with jax.named_scope("coupled_over_h"):
        near = swap(total, "h", n_h, 1) if n_h > 1 else jnp.zeros_like(total)
        (total,) = call(add_kernel, [((128, 128), F32)], ADD_COST)(total, near)
    with jax.named_scope("kv_over_y"):
        (pair,) = call(pair_kernel, [((2, 272, 256), BF16)], PAIR_COST)(
            kvpay, swap(kvpay, "y", NY, 2), total
        )
        other = swap(pair, "y", NY, 1)
    with jax.named_scope("coupled_over_x"):
        if n_x > 1:
            parts = [swap(total, "x", n_x, k) for k in (1, 2, 3)]
        else:
            parts = [jnp.zeros_like(total)] * 3
    with jax.named_scope("join"):
        (kva,) = call(join_kernel, [((NY, 272, 256), BF16)], JOIN_COST)(pair, other, *parts)
    with jax.named_scope("kv_over_core"):
        kvb = swap(kva, "c", NC, 1)
    with jax.named_scope("stats"):
        pay, prob, top = call(
            stats_kernel,
            [((NZ, 176, 128), BF16), ((2, 1024, 1024), BF16), ((16, 128), F32)],
            1_000_000_000,
            [pltpu.VMEM((4, 256, 512), F32), pltpu.VMEM((48, 128), F32)],
            limit=24,
        )(qg, kva, kvb, total, *parts, latent.T, projection, attention_out)
    with jax.named_scope("upstream_over_z"):
        gathered = lax.all_to_all(pay, "z", 0, 0, axis_index_groups=RING_P)
    with jax.named_scope("main"):
        dq, da, db = call(
            main_kernel,
            [((NZ, 128, 256), BF16), ((NY, 256, 256), BF16), ((NY, 256, 256), BF16)],
            4_000_000_000,
            [pltpu.VMEM((1024, 1024), BF16)],
            limit=24,
        )(qg, kva, kvb, gathered, projection, prob, top)
    with jax.named_scope("dkv_over_core"):
        other = swap(db, "c", NC, 1)
        own, *send = call(
            fold_kernel, [((256, 256), F32)] + [((256, 256), BF16)] * 3, FOLD_COST
        )(da, other)
    with jax.named_scope("dkv_over_y"):
        back = [swap(s, "y", NY, k) for k, s in zip((3, 2, 1), (send[2], send[1], send[0]))]
    with jax.named_scope("dq_over_z"):
        dqs = lax.all_to_all(dq, "z", 0, 0, axis_index_groups=RING_D)
    with jax.named_scope("final"):
        return tuple(
            call(final_kernel, [((128, 256), BF16)] * 3, 1_000_000)(own, *back, dqs)
        )


def solution(mesh):
    n_h = min(2, mesh.shape["tp"])
    n_x = mesh.shape["tp"] // n_h
    fine = Mesh(mesh.devices.reshape(NY, NZ, NC, n_x, n_h), ("y", "z", "c", "x", "h"))
    ctx = ("y", "z", "c")
    tp = ("x", "h")
    placed = (
        P(ctx, None),
        P(ctx),
        P(ctx, tp),
        P(ctx, tp),
        P(ctx, tp),
        P(ctx, tp),
        P(tp, None),
    )
    return jax.shard_map(
        functools.partial(local, n_x, n_h),
        mesh=fine,
        in_specs=placed,
        out_specs=(P(ctx, tp), P(ctx, tp), P(ctx, tp)),
        check_vma=False,
    )
```

```python
import functools

import jax
import jax.numpy as jnp
from jax import lax
from jax.experimental import pallas as pl
from jax.experimental.pallas import tpu as pltpu
from jax.sharding import Mesh, PartitionSpec as P

HEAD = 128
SPAN = 64
NZ, NY, NC = 8, 4, 2
LOG2E = 1.4426950408889634
FACTOR = HEAD ** (-0.5)
SCALE = FACTOR * LOG2E
MASKED = -(2.0**100)
F32 = jnp.float32
BF16 = jnp.bfloat16
NT = (((1,), (1,)), ((), ()))
MIB = 1 << 20
RING_Q = [[0, 1, 2, 3, 4, 5, 6, 7]]
RING_P = [[7, 6, 5, 4, 3, 2, 1, 0]]
RING_D = [[0, 1, 2, 3, 4, 5, 6, 7]]
ORDER = (7, 6, 5, 4, 3, 2, 1, 0)
BACK = (0, 1, 2, 3, 4, 5, 6, 7)
JOIN_COST = 1_000_000
PAIR_COST = 5_000_000_000
SUM_COST = 7_000_000_000
ADD_COST = 1_000_000_000
FOLD_COST = 20_000_000_000


def dot_nt(a, b):
    return lax.dot_general(a, b, NT, preferred_element_type=F32)


def dot(a, b):
    return jnp.dot(a, b, preferred_element_type=F32)


def prep_kernel(
    pos_ref, q_hbm, k_hbm, v_hbm, o_hbm, proj_hbm, qpay_ref, kvpay_ref, part_ref, *scratch
):
    buffers, sems = scratch[:-1], scratch[-1]
    sources = (k_hbm, v_hbm, q_hbm, o_hbm, proj_hbm)
    copies = [
        pltpu.make_async_copy(src, dst, sems.at[n])
        for n, (src, dst) in enumerate(zip(sources, buffers))
    ]
    for copy in copies:
        copy.start()
    k_ref, v_ref, q_ref, o_ref, proj_ref = buffers
    block = lax.shift_right_logical(pos_ref[0], 6).astype(F32)
    tag = jnp.full((16, 256), block, F32).astype(BF16)
    for copy in copies:
        copy.wait()
    k, v, q = k_ref[...], v_ref[...], q_ref[...]
    kvpay_ref[0:128, :] = k
    kvpay_ref[128:256, :] = v
    kvpay_ref[256:272, :] = tag
    for i in range(NZ):
        qpay_ref[i, 0:128, :] = q
        qpay_ref[i, 128:144, :] = tag
    part_ref[...] = dot(o_ref[...], proj_ref[...])


def query_positions(qg_ref):
    lane = lax.broadcasted_iota(jnp.int32, (1, 128), 1)
    low = lane < SPAN
    row = (lane & (SPAN - 1)).astype(F32)
    early, late = [], []
    for p in range(NZ // 2):
        first = qg_ref[2 * p, 128:144, 0:128].astype(F32)[0:1, :]
        second = qg_ref[2 * p + 1, 128:144, 0:128].astype(F32)[0:1, :]
        block = jnp.where(low, first, second)
        early.append(block * SPAN + row)
        late.append((127.0 - block) * SPAN + row)
    return jnp.concatenate(early, axis=1), jnp.concatenate(late, axis=1)


def key_positions(kv_ref, late):
    row = lax.broadcasted_iota(jnp.int32, (SPAN, 128), 0).astype(F32)
    out = []
    for j in range(NY):
        block = kv_ref[j, 256:272, 0:128].astype(F32)[0:1, :]
        base = (127.0 - block) * SPAN if late else block * SPAN
        out.append(base + row)
    column = jnp.concatenate(out, axis=0)
    return jnp.concatenate([column] * 4, axis=1)


def rows_of(ref, start, head):
    part = ref[:, start : start + SPAN, head * HEAD : (head + 1) * HEAD]
    return part.reshape(part.shape[0] * SPAN, HEAD)


def stats_kernel(
    qg_ref, kva_ref, kvb_ref, coupled_ref, lat_ref, proj_ref, o_ref,
    out_ref, prob_ref, top_ref, s_ref, tail_ref,
):
    tail_ref[...] = jnp.zeros((48, 128), F32)
    q_early, q_late = query_positions(qg_ref)
    sides = (kva_ref, kvb_ref)
    for head in range(2):
        for part in range(2):
            q = rows_of(qg_ref, part * SPAN, head)
            top = None
            units = []
            for n, kv in enumerate(sides):
                units.append((n, kv, 0, part == 0))
                if part == 1:
                    units.append((n + 2, kv, SPAN, True))
            for slot, kv, start, masked in units:
                s = dot_nt(rows_of(kv, start, head), q) * SCALE
                if masked:
                    qp = q_late if start else q_early
                    s = jnp.where(key_positions(kv, start > 0) <= qp, s, MASKED)
                s_ref[slot] = s
                here = jnp.max(s.reshape(32, 8, 512), axis=0)
                top = here if top is None else jnp.maximum(top, here)
            top = jnp.max(top, axis=0, keepdims=True)
            total = jnp.zeros((8, 512), F32)
            for slot, kv, start, masked in units:
                p = jnp.exp2(s_ref[slot] - top)
                total = total + jnp.sum(p.reshape(32, 8, 512), axis=0)
                rows = slice(slot * 256, (slot + 1) * 256)
                prob_ref[head, rows, part * 512 : (part + 1) * 512] = p.astype(BF16)
            total = jnp.sum(total, axis=0, keepdims=True)
            lse = top + jnp.log(total) * LOG2E
            high = lse.astype(BF16).astype(F32)
            low = lse - high
            group = head * 2 + part
            for r in range(4):
                lanes = slice(r * 128, (r + 1) * 128)
                top_ref[group * 4 + r : group * 4 + r + 1, :] = top[:, lanes]
                row = 8 + group * 8 + r
                tail_ref[row : row + 1, :] = high[:, lanes]
                tail_ref[row + 4 : row + 5, :] = low[:, lanes]
    coupled = coupled_ref[...]
    shifts = coupled[:, 0:64]
    log_scale = coupled[:, 64:128]
    damping = jnp.exp(-log_scale)
    normed = (lat_ref[...].T - shifts) * damping
    upstream = jnp.concatenate([-normed * damping, 1.0 - normed * normed], axis=1).astype(BF16)
    for head in range(2):
        cols = slice(head * HEAD, (head + 1) * HEAD)
        grad = dot_nt(upstream, proj_ref[cols, :]).astype(BF16)
        product = grad.astype(F32) * o_ref[:, cols].astype(F32)
        delta = jnp.sum(product.T, axis=0, keepdims=True)
        high = delta.astype(BF16).astype(F32)
        tail_ref[2 * head : 2 * head + 1, :] = high
        tail_ref[2 * head + 1 : 2 * head + 2, :] = delta - high
    tail = tail_ref[...].astype(BF16)
    for i in range(NZ):
        out_ref[i, 0:128, :] = upstream
        out_ref[i, 128:176, :] = tail


def add_kernel(a_ref, b_ref, out_ref):
    out_ref[...] = a_ref[...] + b_ref[...]


def sum_kernel(a_ref, b_ref, c_ref, d_ref, out_ref):
    out_ref[...] = (a_ref[...] + b_ref[...]) + (c_ref[...] + d_ref[...])


def pair_kernel(own_ref, far_ref, after_ref, out_ref):
    del after_ref
    out_ref[0] = own_ref[...]
    out_ref[1] = far_ref[...]


def join_kernel(own_ref, recv_ref, *refs):
    kv_ref = refs[-1]
    for n in range(2):
        kv_ref[2 * n] = own_ref[n]
        kv_ref[2 * n + 1] = recv_ref[n]


def main_kernel(
    qg_ref, kva_ref, kvb_ref, g_ref, proj_ref, prob_ref, top_ref, dq_ref, da_ref, db_ref, ds_ref
):
    low = lax.broadcasted_iota(jnp.int32, (1, 128), 1) < SPAN
    upstream = [
        jnp.concatenate([g_ref[i, part * SPAN : (part + 1) * SPAN, :] for i in ORDER], axis=0)
        for part in range(2)
    ]
    tails = g_ref[:, 128:176, :].astype(F32)
    deltas = [tails[i, 0:8, :] for i in ORDER]
    turned = [pltpu.roll(t, SPAN, 1) for t in deltas]
    sides = (kva_ref, kvb_ref)
    grads = (da_ref, db_ref)
    for head in range(2):
        cols = slice(head * HEAD, (head + 1) * HEAD)
        proj = proj_ref[cols, :]
        delta, q, dout = [], [], []
        for part in range(2):
            group = head * 2 + part
            row = 8 + group * 8
            partial = tails[:, row : row + 4, :] + tails[:, row + 4 : row + 8, :]
            top = jnp.max(partial, axis=0)
            total = jnp.sum(jnp.exp2(partial - top[None]), axis=0)
            lse = top + jnp.log(total) * LOG2E
            weight = jnp.exp2(top_ref[group * 4 : group * 4 + 4, :] - lse)
            lanes, column = [], []
            for p in range(NZ // 2):
                left = (deltas if part == 0 else turned)[2 * p]
                right = (turned if part == 0 else deltas)[2 * p + 1]
                both = jnp.where(low, left, right)
                here = both[2 * head : 2 * head + 1, :] + both[2 * head + 1 : 2 * head + 2, :]
                lanes.append(here * weight[p : p + 1, :])
                column.append(jnp.broadcast_to(weight[p : p + 1, :], (128, 128)).T)
            delta.append(jnp.concatenate(lanes, axis=1))
            q.append(rows_of(qg_ref, part * SPAN, head))
            grad = dot_nt(upstream[part], proj).astype(BF16).astype(F32)
            dout.append((grad * jnp.concatenate(column, axis=0)).astype(BF16))
        q_all = jnp.concatenate(q, axis=0)
        dout_all = jnp.concatenate(dout, axis=0)

        def unit(rows, part, values):
            span = slice(part * 512, (part + 1) * 512)
            p = prob_ref[head, rows, span].astype(F32)
            ds_ref[rows, span] = (p * (dot_nt(values, dout[part]) - delta[part])).astype(BF16)

        for n in range(2):
            kv, grad = sides[n], grads[n]
            rows = slice(n * 256, (n + 1) * 256)
            values = rows_of(kv, 128, head)
            unit(rows, 0, values)
            unit(rows, 1, values)
            dv = dot(prob_ref[head, rows, :], dout_all)
            dk = dot(ds_ref[rows, :], q_all)
            grad[:, 0:64, cols] = (dk * FACTOR).astype(BF16).reshape(NY, SPAN, HEAD)
            grad[:, 128:192, cols] = dv.astype(BF16).reshape(NY, SPAN, HEAD)
            rows = slice(512 + n * 256, 512 + (n + 1) * 256)
            unit(rows, 1, rows_of(kv, 192, head))
            dv = dot(prob_ref[head, rows, 512:1024], dout[1])
            dk = dot(ds_ref[rows, 512:1024], q[1])
            grad[:, 64:128, cols] = (dk * FACTOR).astype(BF16).reshape(NY, SPAN, HEAD)
            grad[:, 192:256, cols] = dv.astype(BF16).reshape(NY, SPAN, HEAD)
        early_t = jnp.concatenate([rows_of(kv, 0, head) for kv in sides], axis=0).T
        late_t = jnp.concatenate([rows_of(kv, 64, head) for kv in sides], axis=0).T
        dqe = dot(early_t, ds_ref[0:512, 0:512])
        dql = dot(early_t, ds_ref[0:512, 512:1024]) + dot(late_t, ds_ref[512:1024, 512:1024])
        dqe = (dqe * FACTOR).T.astype(BF16)
        dql = (dql * FACTOR).T.astype(BF16)
        for i, place in enumerate(BACK):
            dq_ref[place, 0:64, cols] = dqe[i * SPAN : (i + 1) * SPAN, :]
            dq_ref[place, 64:128, cols] = dql[i * SPAN : (i + 1) * SPAN, :]


def fold_kernel(own_ref, recv_ref, o0_ref, o1_ref, o2_ref, o3_ref):
    o0_ref[...] = own_ref[0].astype(F32) + recv_ref[0].astype(F32)
    for k, ref in ((1, o1_ref), (2, o2_ref), (3, o3_ref)):
        ref[...] = (own_ref[k].astype(F32) + recv_ref[k].astype(F32)).astype(BF16)


def final_kernel(own_ref, r1_ref, r2_ref, r3_ref, dq_ref, qo_ref, ko_ref, vo_ref):
    total = own_ref[...]
    for ref in (r1_ref, r2_ref, r3_ref):
        total = total + ref[...].astype(F32)
    ko_ref[...] = total[0:128, :].astype(BF16)
    vo_ref[...] = total[128:256, :].astype(BF16)
    dq = dq_ref[0].astype(F32)
    for i in range(1, NZ):
        dq = dq + dq_ref[i].astype(F32)
    qo_ref[...] = dq.astype(BF16)


def call(kernel, outs, cost, scratch=(), specs=None, limit=48):
    vmem = pl.BlockSpec(memory_space=pltpu.VMEM)

    def run(*args):
        return pl.pallas_call(
            kernel,
            out_shape=[jax.ShapeDtypeStruct(s, d) for s, d in outs],
            in_specs=specs or [vmem] * len(args),
            out_specs=[vmem] * len(outs),
            scratch_shapes=list(scratch),
            compiler_params=pltpu.CompilerParams(vmem_limit_bytes=limit * MIB),
            cost_estimate=pl.CostEstimate(flops=cost, bytes_accessed=2 * MIB, transcendentals=0),
        )(*args)

    return run


def swap(x, axis, size, k):
    return lax.ppermute(x, axis, [(i, i ^ k) for i in range(size)])


def local(n_x, n_h, latent, positions, queries, keys, values, attention_out, projection):
    with jax.named_scope("prep"):
        qpay, kvpay, total = call(
            prep_kernel,
            [((NZ, 144, 256), BF16), ((272, 256), BF16), ((128, 128), F32)],
            10_000_000,
            [pltpu.VMEM((128, 256), BF16)] * 4
            + [pltpu.VMEM((256, 128), BF16), pltpu.SemaphoreType.DMA((5,))],
            [pl.BlockSpec(memory_space=pltpu.SMEM)] + [pl.BlockSpec(memory_space=pltpu.HBM)] * 5,
            limit=62,
        )(positions, queries, keys, values, attention_out, projection)
    with jax.named_scope("q_over_z"):
        qg = lax.all_to_all(qpay, "z", 0, 0, axis_index_groups=RING_Q)
    with jax.named_scope("coupled_over_h"):
        near = swap(total, "h", n_h, 1) if n_h > 1 else jnp.zeros_like(total)
        (total,) = call(add_kernel, [((128, 128), F32)], ADD_COST)(total, near)
    with jax.named_scope("kv_over_y"):
        (pair,) = call(pair_kernel, [((2, 272, 256), BF16)], PAIR_COST)(
            kvpay, swap(kvpay, "y", NY, 2), total
        )
        other = swap(pair, "y", NY, 1)
    with jax.named_scope("coupled_over_x"):
        if n_x > 1:
            parts = [swap(total, "x", n_x, k) for k in (1, 2, 3)]
        else:
            parts = [jnp.zeros_like(total)] * 3
    with jax.named_scope("join"):
        (kva,) = call(join_kernel, [((NY, 272, 256), BF16)], JOIN_COST)(pair, other)
    with jax.named_scope("kv_over_core"):
        kvb = swap(kva, "c", NC, 1)
    with jax.named_scope("coupled_over_x"):
        (coupled,) = call(sum_kernel, [((128, 128), F32)], SUM_COST)(total, *parts)
    with jax.named_scope("stats"):
        pay, prob, top = call(
            stats_kernel,
            [((NZ, 176, 128), BF16), ((2, 1024, 1024), BF16), ((16, 128), F32)],
            1_000_000_000,
            [pltpu.VMEM((4, 256, 512), F32), pltpu.VMEM((48, 128), F32)],
            limit=24,
        )(qg, kva, kvb, coupled, latent.T, projection, attention_out)
    with jax.named_scope("upstream_over_z"):
        gathered = lax.all_to_all(pay, "z", 0, 0, axis_index_groups=RING_P)
    with jax.named_scope("main"):
        dq, da, db = call(
            main_kernel,
            [((NZ, 128, 256), BF16), ((NY, 256, 256), BF16), ((NY, 256, 256), BF16)],
            4_000_000_000,
            [pltpu.VMEM((1024, 1024), BF16)],
            limit=24,
        )(qg, kva, kvb, gathered, projection, prob, top)
    with jax.named_scope("dkv_over_core"):
        other = swap(db, "c", NC, 1)
        own, *send = call(
            fold_kernel, [((256, 256), F32)] + [((256, 256), BF16)] * 3, FOLD_COST
        )(da, other)
    with jax.named_scope("dkv_over_y"):
        back = [swap(s, "y", NY, k) for k, s in zip((3, 2, 1), (send[2], send[1], send[0]))]
    with jax.named_scope("dq_over_z"):
        dqs = lax.all_to_all(dq, "z", 0, 0, axis_index_groups=RING_D)
    with jax.named_scope("final"):
        return tuple(
            call(final_kernel, [((128, 256), BF16)] * 3, 1_000_000)(own, *back, dqs)
        )


def solution(mesh):
    n_h = min(2, mesh.shape["tp"])
    n_x = mesh.shape["tp"] // n_h
    fine = Mesh(mesh.devices.reshape(NY, NZ, NC, n_x, n_h), ("y", "z", "c", "x", "h"))
    ctx = ("y", "z", "c")
    tp = ("x", "h")
    placed = (
        P(ctx, None),
        P(ctx),
        P(ctx, tp),
        P(ctx, tp),
        P(ctx, tp),
        P(ctx, tp),
        P(tp, None),
    )
    return jax.shard_map(
        functools.partial(local, n_x, n_h),
        mesh=fine,
        in_specs=placed,
        out_specs=(P(ctx, tp), P(ctx, tp), P(ctx, tp)),
        check_vma=False,
    )
```

```python
import functools

import jax
import jax.numpy as jnp
from jax import lax
from jax.experimental import pallas as pl
from jax.experimental.pallas import tpu as pltpu
from jax.sharding import Mesh, PartitionSpec as P

HEAD = 128
SPAN = 64
NZ, NY, NC = 8, 4, 2
LOG2E = 1.4426950408889634
FACTOR = HEAD ** (-0.5)
SCALE = FACTOR * LOG2E
MASKED = -(2.0**100)
F32 = jnp.float32
BF16 = jnp.bfloat16
NT = (((1,), (1,)), ((), ()))
MIB = 1 << 20
RING_Q = [[0, 1, 2, 3, 4, 5, 6, 7]]
RING_P = [[7, 6, 5, 4, 3, 2, 1, 0]]
RING_D = [[0, 1, 2, 3, 4, 5, 6, 7]]
ORDER = (7, 6, 5, 4, 3, 2, 1, 0)
BACK = (0, 1, 2, 3, 4, 5, 6, 7)
JOIN_COST = 1_000_000
PAIR_COST = 5_000_000_000
SUM_COST = 7_000_000_000
ADD_COST = 1_000_000_000
FOLD_COST = 20_000_000_000


def dot_nt(a, b):
    return lax.dot_general(a, b, NT, preferred_element_type=F32)


def dot(a, b):
    return jnp.dot(a, b, preferred_element_type=F32)


def prep_kernel(
    pos_ref, k_hbm, v_hbm, o_hbm, proj_hbm, kvpay_ref, part_ref, *scratch
):
    buffers, sems = scratch[:-1], scratch[-1]
    sources = (k_hbm, v_hbm, o_hbm, proj_hbm)
    copies = [
        pltpu.make_async_copy(src, dst, sems.at[n])
        for n, (src, dst) in enumerate(zip(sources, buffers))
    ]
    for copy in copies:
        copy.start()
    k_ref, v_ref, o_ref, proj_ref = buffers
    block = lax.shift_right_logical(pos_ref[0], 6).astype(F32)
    tag = jnp.full((16, 256), block, F32).astype(BF16)
    for copy in copies:
        copy.wait()
    k, v = k_ref[...], v_ref[...]
    kvpay_ref[0:128, :] = k
    kvpay_ref[128:256, :] = v
    kvpay_ref[256:272, :] = tag
    part_ref[...] = dot(o_ref[...], proj_ref[...])


def copies_kernel(pos_ref, q_ref, qpay_ref):
    block = lax.shift_right_logical(pos_ref[0], 6).astype(F32)
    tag = jnp.full((16, 256), block, F32).astype(BF16)
    q = q_ref[...]
    for i in range(NZ):
        qpay_ref[i, 0:128, :] = q
        qpay_ref[i, 128:144, :] = tag


def query_positions(qg_ref):
    lane = lax.broadcasted_iota(jnp.int32, (1, 128), 1)
    low = lane < SPAN
    row = (lane & (SPAN - 1)).astype(F32)
    early, late = [], []
    for p in range(NZ // 2):
        first = qg_ref[2 * p, 128:144, 0:128].astype(F32)[0:1, :]
        second = qg_ref[2 * p + 1, 128:144, 0:128].astype(F32)[0:1, :]
        block = jnp.where(low, first, second)
        early.append(block * SPAN + row)
        late.append((127.0 - block) * SPAN + row)
    return jnp.concatenate(early, axis=1), jnp.concatenate(late, axis=1)


def key_positions(kv_ref, late):
    row = lax.broadcasted_iota(jnp.int32, (SPAN, 128), 0).astype(F32)
    out = []
    for j in range(NY):
        block = kv_ref[j, 256:272, 0:128].astype(F32)[0:1, :]
        base = (127.0 - block) * SPAN if late else block * SPAN
        out.append(base + row)
    column = jnp.concatenate(out, axis=0)
    return jnp.concatenate([column] * 4, axis=1)


def rows_of(ref, start, head):
    part = ref[:, start : start + SPAN, head * HEAD : (head + 1) * HEAD]
    return part.reshape(part.shape[0] * SPAN, HEAD)


def stats_kernel(
    qg_ref, kva_ref, kvb_ref, coupled_ref, lat_ref, proj_ref, o_ref,
    out_ref, prob_ref, top_ref, s_ref, tail_ref,
):
    tail_ref[...] = jnp.zeros((48, 128), F32)
    q_early, q_late = query_positions(qg_ref)
    sides = (kva_ref, kvb_ref)
    for head in range(2):
        for part in range(2):
            q = rows_of(qg_ref, part * SPAN, head)
            top = None
            units = []
            for n, kv in enumerate(sides):
                units.append((n, kv, 0, part == 0))
                if part == 1:
                    units.append((n + 2, kv, SPAN, True))
            for slot, kv, start, masked in units:
                s = dot_nt(rows_of(kv, start, head), q) * SCALE
                if masked:
                    qp = q_late if start else q_early
                    s = jnp.where(key_positions(kv, start > 0) <= qp, s, MASKED)
                s_ref[slot] = s
                here = jnp.max(s.reshape(32, 8, 512), axis=0)
                top = here if top is None else jnp.maximum(top, here)
            top = jnp.max(top, axis=0, keepdims=True)
            total = jnp.zeros((8, 512), F32)
            for slot, kv, start, masked in units:
                p = jnp.exp2(s_ref[slot] - top)
                total = total + jnp.sum(p.reshape(32, 8, 512), axis=0)
                rows = slice(slot * 256, (slot + 1) * 256)
                prob_ref[head, rows, part * 512 : (part + 1) * 512] = p.astype(BF16)
            total = jnp.sum(total, axis=0, keepdims=True)
            lse = top + jnp.log(total) * LOG2E
            high = lse.astype(BF16).astype(F32)
            low = lse - high
            group = head * 2 + part
            for r in range(4):
                lanes = slice(r * 128, (r + 1) * 128)
                top_ref[group * 4 + r : group * 4 + r + 1, :] = top[:, lanes]
                row = 8 + group * 8 + r
                tail_ref[row : row + 1, :] = high[:, lanes]
                tail_ref[row + 4 : row + 5, :] = low[:, lanes]
    coupled = coupled_ref[...]
    shifts = coupled[:, 0:64]
    log_scale = coupled[:, 64:128]
    damping = jnp.exp(-log_scale)
    normed = (lat_ref[...].T - shifts) * damping
    upstream = jnp.concatenate([-normed * damping, 1.0 - normed * normed], axis=1).astype(BF16)
    for head in range(2):
        cols = slice(head * HEAD, (head + 1) * HEAD)
        grad = dot_nt(upstream, proj_ref[cols, :]).astype(BF16)
        product = grad.astype(F32) * o_ref[:, cols].astype(F32)
        delta = jnp.sum(product.T, axis=0, keepdims=True)
        high = delta.astype(BF16).astype(F32)
        tail_ref[2 * head : 2 * head + 1, :] = high
        tail_ref[2 * head + 1 : 2 * head + 2, :] = delta - high
    tail = tail_ref[...].astype(BF16)
    for i in range(NZ):
        out_ref[i, 0:128, :] = upstream
        out_ref[i, 128:176, :] = tail


def add_kernel(a_ref, b_ref, out_ref):
    out_ref[...] = a_ref[...] + b_ref[...]


def sum_kernel(a_ref, b_ref, c_ref, d_ref, out_ref):
    out_ref[...] = (a_ref[...] + b_ref[...]) + (c_ref[...] + d_ref[...])


def pair_kernel(own_ref, far_ref, after_ref, out_ref):
    del after_ref
    out_ref[0] = own_ref[...]
    out_ref[1] = far_ref[...]


def join_kernel(own_ref, recv_ref, *refs):
    kv_ref = refs[-1]
    for n in range(2):
        kv_ref[2 * n] = own_ref[n]
        kv_ref[2 * n + 1] = recv_ref[n]


def main_kernel(
    qg_ref, kva_ref, kvb_ref, g_ref, proj_ref, prob_ref, top_ref, dq_ref, da_ref, db_ref, ds_ref
):
    low = lax.broadcasted_iota(jnp.int32, (1, 128), 1) < SPAN
    upstream = [
        jnp.concatenate([g_ref[i, part * SPAN : (part + 1) * SPAN, :] for i in ORDER], axis=0)
        for part in range(2)
    ]
    tails = g_ref[:, 128:176, :].astype(F32)
    deltas = [tails[i, 0:8, :] for i in ORDER]
    turned = [pltpu.roll(t, SPAN, 1) for t in deltas]
    sides = (kva_ref, kvb_ref)
    grads = (da_ref, db_ref)
    for head in range(2):
        cols = slice(head * HEAD, (head + 1) * HEAD)
        proj = proj_ref[cols, :]
        delta, q, dout = [], [], []
        for part in range(2):
            group = head * 2 + part
            row = 8 + group * 8
            partial = tails[:, row : row + 4, :] + tails[:, row + 4 : row + 8, :]
            top = jnp.max(partial, axis=0)
            total = jnp.sum(jnp.exp2(partial - top[None]), axis=0)
            lse = top + jnp.log(total) * LOG2E
            weight = jnp.exp2(top_ref[group * 4 : group * 4 + 4, :] - lse)
            lanes, column = [], []
            for p in range(NZ // 2):
                left = (deltas if part == 0 else turned)[2 * p]
                right = (turned if part == 0 else deltas)[2 * p + 1]
                both = jnp.where(low, left, right)
                here = both[2 * head : 2 * head + 1, :] + both[2 * head + 1 : 2 * head + 2, :]
                lanes.append(here * weight[p : p + 1, :])
                column.append(jnp.broadcast_to(weight[p : p + 1, :], (128, 128)).T)
            delta.append(jnp.concatenate(lanes, axis=1))
            q.append(rows_of(qg_ref, part * SPAN, head))
            grad = dot_nt(upstream[part], proj).astype(BF16).astype(F32)
            dout.append((grad * jnp.concatenate(column, axis=0)).astype(BF16))
        q_all = jnp.concatenate(q, axis=0)
        dout_all = jnp.concatenate(dout, axis=0)

        def unit(rows, part, values):
            span = slice(part * 512, (part + 1) * 512)
            p = prob_ref[head, rows, span].astype(F32)
            ds_ref[rows, span] = (p * (dot_nt(values, dout[part]) - delta[part])).astype(BF16)

        for n in range(2):
            kv, grad = sides[n], grads[n]
            rows = slice(n * 256, (n + 1) * 256)
            values = rows_of(kv, 128, head)
            unit(rows, 0, values)
            unit(rows, 1, values)
            dv = dot(prob_ref[head, rows, :], dout_all)
            dk = dot(ds_ref[rows, :], q_all)
            grad[:, 0:64, cols] = (dk * FACTOR).astype(BF16).reshape(NY, SPAN, HEAD)
            grad[:, 128:192, cols] = dv.astype(BF16).reshape(NY, SPAN, HEAD)
            rows = slice(512 + n * 256, 512 + (n + 1) * 256)
            unit(rows, 1, rows_of(kv, 192, head))
            dv = dot(prob_ref[head, rows, 512:1024], dout[1])
            dk = dot(ds_ref[rows, 512:1024], q[1])
            grad[:, 64:128, cols] = (dk * FACTOR).astype(BF16).reshape(NY, SPAN, HEAD)
            grad[:, 192:256, cols] = dv.astype(BF16).reshape(NY, SPAN, HEAD)
        early_t = jnp.concatenate([rows_of(kv, 0, head) for kv in sides], axis=0).T
        late_t = jnp.concatenate([rows_of(kv, 64, head) for kv in sides], axis=0).T
        dqe = dot(early_t, ds_ref[0:512, 0:512])
        dql = dot(early_t, ds_ref[0:512, 512:1024]) + dot(late_t, ds_ref[512:1024, 512:1024])
        dqe = (dqe * FACTOR).T.astype(BF16)
        dql = (dql * FACTOR).T.astype(BF16)
        for i, place in enumerate(BACK):
            dq_ref[place, 0:64, cols] = dqe[i * SPAN : (i + 1) * SPAN, :]
            dq_ref[place, 64:128, cols] = dql[i * SPAN : (i + 1) * SPAN, :]


def fold_kernel(own_ref, recv_ref, o0_ref, o1_ref, o2_ref, o3_ref):
    o0_ref[...] = own_ref[0].astype(F32) + recv_ref[0].astype(F32)
    for k, ref in ((1, o1_ref), (2, o2_ref), (3, o3_ref)):
        ref[...] = (own_ref[k].astype(F32) + recv_ref[k].astype(F32)).astype(BF16)


def final_kernel(own_ref, r1_ref, r2_ref, r3_ref, dq_ref, qo_ref, ko_ref, vo_ref):
    total = own_ref[...]
    for ref in (r1_ref, r2_ref, r3_ref):
        total = total + ref[...].astype(F32)
    ko_ref[...] = total[0:128, :].astype(BF16)
    vo_ref[...] = total[128:256, :].astype(BF16)
    dq = dq_ref[0].astype(F32)
    for i in range(1, NZ):
        dq = dq + dq_ref[i].astype(F32)
    qo_ref[...] = dq.astype(BF16)


def call(kernel, outs, cost, scratch=(), specs=None, limit=48):
    vmem = pl.BlockSpec(memory_space=pltpu.VMEM)

    def run(*args):
        return pl.pallas_call(
            kernel,
            out_shape=[jax.ShapeDtypeStruct(s, d) for s, d in outs],
            in_specs=specs or [vmem] * len(args),
            out_specs=[vmem] * len(outs),
            scratch_shapes=list(scratch),
            compiler_params=pltpu.CompilerParams(vmem_limit_bytes=limit * MIB),
            cost_estimate=pl.CostEstimate(flops=cost, bytes_accessed=2 * MIB, transcendentals=0),
        )(*args)

    return run


def swap(x, axis, size, k):
    return lax.ppermute(x, axis, [(i, i ^ k) for i in range(size)])


def local(n_x, n_h, latent, positions, queries, keys, values, attention_out, projection):
    with jax.named_scope("prep"):
        kvpay, total = call(
            prep_kernel,
            [((272, 256), BF16), ((128, 128), F32)],
            10_000_000,
            [pltpu.VMEM((128, 256), BF16)] * 3
            + [pltpu.VMEM((256, 128), BF16), pltpu.SemaphoreType.DMA((4,))],
            [pl.BlockSpec(memory_space=pltpu.SMEM)] + [pl.BlockSpec(memory_space=pltpu.HBM)] * 4,
            limit=62,
        )(positions, keys, values, attention_out, projection)
    with jax.named_scope("q_copies"):
        (qpay,) = call(
            copies_kernel,
            [((NZ, 144, 256), BF16)],
            1_000_000,
            specs=[pl.BlockSpec(memory_space=m) for m in (pltpu.SMEM, pltpu.VMEM)],
        )(positions, queries)
    with jax.named_scope("q_over_z"):
        qg = lax.all_to_all(qpay, "z", 0, 0, axis_index_groups=RING_Q)
    with jax.named_scope("coupled_over_h"):
        near = swap(total, "h", n_h, 1) if n_h > 1 else jnp.zeros_like(total)
        (total,) = call(add_kernel, [((128, 128), F32)], ADD_COST)(total, near)
    with jax.named_scope("kv_over_y"):
        (pair,) = call(pair_kernel, [((2, 272, 256), BF16)], PAIR_COST)(
            kvpay, swap(kvpay, "y", NY, 2), total
        )
        other = swap(pair, "y", NY, 1)
    with jax.named_scope("coupled_over_x"):
        if n_x > 1:
            parts = [swap(total, "x", n_x, k) for k in (1, 2, 3)]
        else:
            parts = [jnp.zeros_like(total)] * 3
    with jax.named_scope("join"):
        (kva,) = call(join_kernel, [((NY, 272, 256), BF16)], JOIN_COST)(pair, other)
    with jax.named_scope("kv_over_core"):
        kvb = swap(kva, "c", NC, 1)
    with jax.named_scope("coupled_over_x"):
        (coupled,) = call(sum_kernel, [((128, 128), F32)], SUM_COST)(total, *parts)
    with jax.named_scope("stats"):
        pay, prob, top = call(
            stats_kernel,
            [((NZ, 176, 128), BF16), ((2, 1024, 1024), BF16), ((16, 128), F32)],
            1_000_000_000,
            [pltpu.VMEM((4, 256, 512), F32), pltpu.VMEM((48, 128), F32)],
            limit=24,
        )(qg, kva, kvb, coupled, latent.T, projection, attention_out)
    with jax.named_scope("upstream_over_z"):
        gathered = lax.all_to_all(pay, "z", 0, 0, axis_index_groups=RING_P)
    with jax.named_scope("main"):
        dq, da, db = call(
            main_kernel,
            [((NZ, 128, 256), BF16), ((NY, 256, 256), BF16), ((NY, 256, 256), BF16)],
            4_000_000_000,
            [pltpu.VMEM((1024, 1024), BF16)],
            limit=24,
        )(qg, kva, kvb, gathered, projection, prob, top)
    with jax.named_scope("dkv_over_core"):
        other = swap(db, "c", NC, 1)
        own, *send = call(
            fold_kernel, [((256, 256), F32)] + [((256, 256), BF16)] * 3, FOLD_COST
        )(da, other)
    with jax.named_scope("dkv_over_y"):
        back = [swap(s, "y", NY, k) for k, s in zip((3, 2, 1), (send[2], send[1], send[0]))]
    with jax.named_scope("dq_over_z"):
        dqs = lax.all_to_all(dq, "z", 0, 0, axis_index_groups=RING_D)
    with jax.named_scope("final"):
        return tuple(
            call(final_kernel, [((128, 256), BF16)] * 3, 1_000_000)(own, *back, dqs)
        )


def solution(mesh):
    n_h = min(2, mesh.shape["tp"])
    n_x = mesh.shape["tp"] // n_h
    fine = Mesh(mesh.devices.reshape(NY, NZ, NC, n_x, n_h), ("y", "z", "c", "x", "h"))
    ctx = ("y", "z", "c")
    tp = ("x", "h")
    placed = (
        P(ctx, None),
        P(ctx),
        P(ctx, tp),
        P(ctx, tp),
        P(ctx, tp),
        P(ctx, tp),
        P(tp, None),
    )
    return jax.shard_map(
        functools.partial(local, n_x, n_h),
        mesh=fine,
        in_specs=placed,
        out_specs=(P(ctx, tp), P(ctx, tp), P(ctx, tp)),
        check_vma=False,
    )
```
